32 devices in a mesh: cluster: 8 (over z, y), feat: 4 (over x, core).
Axes of the slice: x: 2, y: 2, z: 4, core: 2. Of those that a mesh axis runs over, the one named last changes fastest.
Arguments:
- queries: bfloat16 [2048, 1024], P('cluster', 'feat'), may hold values from -6 to 6
- assign: int32 [2048, 1], P('cluster'), may hold values from 0 to 7, as said below
- band_mask: int32 [8, 7], replicated, may hold values from 0 to 1, as said below
- keys: bfloat16 [4096, 1024], P(('cluster', 'feat')), may hold values from -6 to 6
- labels: bfloat16 [4096, 1000], P(('cluster', 'feat')), may hold values from -24 to 24
- prior: bfloat16 [4096], P(('cluster', 'feat')), may hold values from -2 to 506
Outputs:
- propagated: bfloat16 [2048, 1000], P('cluster', 'feat')
The draws below stay inside these ranges and needn't reach their ends.
Inputs may be any that keep to these rules, and one draw needn't show every extreme that they name: `assign`: in each aligned block of 256 rows at most 64 rows name one cluster. `band_mask`: entry 3 of every row is 1.
All inputs are finite; a program needn't handle non-finite values.
Results may differ from the reference program's by a relative error of at most 0.014.
Values may be sent and summed in bfloat16 or wider, within the bound.
A program may use at most 64 MiB of HBM per device.

```python
import math
import jax
import jax.numpy as jnp
from jax import lax

D = 1024
CLASSES = 1000
Q_DEV = 256
CB = 128
REACH = 3
BAND = 7
CLUSTERS = 8
CAP = 64
QUERIES = 2048
CORPUS = 4096


def key_table(key):
    return jnp.clip(jax.random.normal(jax.random.fold_in(key, 11), (CORPUS, D), jnp.float32), -6.0, 6.0)


def mask_table(key):
    coins = jax.random.randint(jax.random.fold_in(key, 13), (CLUSTERS, BAND), 0, 4)
    centre = jnp.arange(BAND)[None, :] == REACH
    return jnp.where(centre | (coins > 0), 1, 0).astype(jnp.int32)


def assign_block(block_key):
    hottest = jax.random.randint(jax.random.fold_in(block_key, 1), (), 0, CLUSTERS)
    order = jax.random.permutation(jax.random.fold_in(block_key, 2), CLUSTERS * CAP)
    owner = order // CAP
    ranked = jnp.where(owner == hottest, CLUSTERS * CAP, 0) + jnp.arange(CLUSTERS * CAP)
    others = owner[jnp.argsort(ranked)][:Q_DEV - CAP]
    rows_all = jnp.concatenate([jnp.full((CAP,), hottest, jnp.int32), others.astype(jnp.int32)])
    shuffle = jax.random.permutation(jax.random.fold_in(block_key, 3), Q_DEV)
    return rows_all[shuffle]


def assign_table(key):
    block_keys = jax.random.split(jax.random.fold_in(key, 31), CLUSTERS)
    return jax.vmap(assign_block)(block_keys).reshape(QUERIES).astype(jnp.int32)


def draw_band_mask(key, part):
    return mask_table(key)


def draw_assign(key, part):
    return assign_table(key).reshape(QUERIES, 1)


def draw_keys(key, part):
    return key_table(key).astype(jnp.bfloat16)


def draw_queries(key, part):
    base = jnp.clip(jax.random.normal(jax.random.fold_in(key, 41), (QUERIES, D), jnp.float32), -6.0, 6.0)
    home = assign_table(key)
    band_table = mask_table(key)
    picked = jax.random.randint(jax.random.fold_in(key, 43), (QUERIES,), 0, BAND)
    alive = band_table[home, picked] > 0
    offset = jnp.where(alive, picked, REACH) - REACH
    cluster = (home + offset) % CLUSTERS
    per_cluster = CORPUS // CLUSTERS
    device = jax.random.randint(jax.random.fold_in(key, 47), (QUERIES,), 0, per_cluster // CB)
    row_index = (cluster * per_cluster + device * CB).astype(jnp.int32)
    aligned = jnp.clip(3.0 * key_table(key)[row_index], -6.0, 6.0)
    chosen = jax.random.randint(jax.random.fold_in(key, 53), (QUERIES,), 0, 8) == 0
    return jnp.where(chosen[:, None], aligned, base).astype(jnp.bfloat16)


def draw_prior(key, part):
    base = jnp.clip(jax.random.normal(jax.random.fold_in(key, 51), (CORPUS,), jnp.float32) * 0.6, -2.0, 2.0)
    return base.astype(jnp.bfloat16)


def steps_of(rng, extent, cuts, least, top_value):
    gain, own = 1.0, jax.random.fold_in(rng, 6)
    for dim, parts in cuts:
        steps = jnp.exp(jax.random.uniform(jax.random.fold_in(own, dim), (parts,), jnp.float32, least / len(cuts), top_value / len(cuts)))
        gain = gain * jnp.repeat(steps, extent[dim] // parts).reshape([-1 if axis == dim else 1 for axis in range(len(extent))])
    return gain


def noise(own_key, dims, deviation, limit, shards=(), kind=jnp.bfloat16):
    result = jax.random.normal(own_key, dims, jnp.float32) * deviation
    if len(shards) > 0:
        result = steps_of(own_key, dims, shards, -0.22, 0.18) * result
    return jnp.clip(result, min=-limit, max=limit).astype(kind)


def setup_inputs(seed: int = 0) -> dict:
    arg_keys = jax.random.split(jax.random.key(seed), 7)
    queries = draw_queries(jax.random.fold_in(arg_keys[6], 71), 0)
    assign = draw_assign(jax.random.fold_in(arg_keys[6], 71), 0)
    band_mask = draw_band_mask(jax.random.fold_in(arg_keys[6], 71), 0)
    keys = draw_keys(jax.random.fold_in(arg_keys[6], 71), 0)
    labels = noise(arg_keys[4], (CORPUS, CLASSES), 4.0, 24.0, ((0, 32),))
    prior = draw_prior(jax.random.fold_in(arg_keys[6], 71), 0)
    return {"queries": queries, "assign": assign, "band_mask": band_mask, "keys": keys, "labels": labels, "prior": prior}


def reference(queries, assign, band_mask, keys, labels, prior):
    capacity = 2 * Q_DEV // CLUSTERS
    slots = CLUSTERS * capacity
    target = assign[:, 0].astype(jnp.int32)
    onehot = (target[:, None] == jnp.arange(CLUSTERS, dtype=jnp.int32)[None, :]).astype(jnp.int32)
    before = jnp.cumsum(onehot, axis=0) - onehot
    position = (target * slots + lax.optimization_barrier(jnp.sum(before * onehot, axis=1))).astype(jnp.int32)
    grouped = jnp.zeros((CLUSTERS * slots, D), queries.dtype).at[position].set(queries)
    grouped = grouped.reshape(CLUSTERS, slots, D)
    per_cluster = CORPUS // CLUSTERS
    key_blocks = keys.reshape(CLUSTERS, per_cluster, D)
    label_blocks = labels.reshape(CLUSTERS, per_cluster, CLASSES)
    prior_blocks = prior.reshape(CLUSTERS, per_cluster)
    offsets = jnp.arange(-REACH, REACH + 1, dtype=jnp.int32)
    scale = 2.0 / math.sqrt(D)

    def score_cluster(cluster):
        chosen = ((cluster + offsets) % CLUSTERS).astype(jnp.int32)
        band_keys = jnp.take(key_blocks, chosen, axis=0).reshape(BAND * per_cluster, D)
        band_labels = jnp.take(label_blocks, chosen, axis=0).reshape(BAND * per_cluster, CLASSES)
        band_prior = jnp.take(prior_blocks, chosen, axis=0).reshape(BAND * per_cluster)
        live = jnp.repeat(band_mask[cluster] > 0, per_cluster)
        scores = jnp.dot(grouped[cluster], band_keys.T, preferred_element_type=jnp.float32) * scale
        scores = scores + band_prior.astype(jnp.float32)[None, :]
        top = lax.optimization_barrier(jnp.max(jnp.where(live[None, :], scores, -jnp.inf), axis=1))
        weight = jnp.where(live[None, :], jnp.exp(scores - top[:, None]), jnp.float32(0.0))
        total = lax.optimization_barrier(jnp.sum(weight, axis=1))
        numer = jnp.dot(weight.astype(jnp.bfloat16), band_labels, preferred_element_type=jnp.float32)
        return (numer / total[:, None]).astype(jnp.bfloat16)
    results = lax.map(score_cluster, jnp.arange(CLUSTERS, dtype=jnp.int32))
    return results.reshape(CLUSTERS * slots, CLASSES)[position]
```

```python
import functools
import math

import jax
import jax.numpy as jnp
from jax import lax
from jax.experimental import pallas as pl
from jax.experimental.pallas import tpu as pltpu
from jax.sharding import PartitionSpec as P

REACH = 3
HIDDEN = -1e30
MESH = pl.DeviceIdType.MESH


temper = 2.0


def spread(row, width):
    return jnp.broadcast_to(row, (width, row.shape[1])).T


def widen(column, times):
    return jnp.concatenate([column] * times, axis=1)


def plane_kernel(
    scale,
    queries_ref,
    assign_ref,
    mask_ref,
    keys_ref,
    labels_ref,
    prior_ref,
    out_ref,
    qbuf,
    vbuf,
    kbuf,
    lbuf,
    pbuf,
    weights,
    stats_own,
    numer_own,
    numer_out,
    numer_in,
    stats_in,
    home_out,
    home_stats_out,
    home_in,
    home_stats_in,
    final_out,
    final_in,
    send_sem,
    recv_sem,
):
    cluster = lax.axis_index("cluster")
    feat = lax.axis_index("feat")
    clusters = mask_ref.shape[0]
    floors = clusters // 2
    half = queries_ref.shape[0] // 2
    rows = keys_ref.shape[0]
    part = labels_ref.shape[1] // 4
    padded = lbuf.shape[1] // 4
    z, y = lax.div(cluster, 2), lax.rem(cluster, 2)
    x, core = lax.div(feat, 2), lax.rem(feat, 2)
    twin = (cluster, feat + 1 - 2 * core)
    across = (cluster, feat + 2 - 4 * x)
    beside = (cluster + 1 - 2 * y, feat)

    def floor_peer(by):
        return (lax.rem(cluster + 2 * by, clusters), feat)

    barrier = pltpu.get_barrier_semaphore()
    peers = [twin, across, beside] + [floor_peer(by) for by in range(1, floors)]
    for peer in peers:
        pl.semaphore_signal(barrier, inc=1, device_id=peer, device_id_type=MESH)
    pl.semaphore_wait(barrier, len(peers))

    started = []

    def send(src, dst, peer):
        index = len(started)
        copy = pltpu.make_async_remote_copy(
            src_ref=src,
            dst_ref=dst,
            send_sem=send_sem.at[index],
            recv_sem=recv_sem.at[index],
            device_id=peer,
            device_id_type=MESH,
        )
        copy.start()
        started.append(copy)
        return copy

    def block(index):
        return pl.ds(index * rows, rows)

    mine = pl.ds(pl.multiple_of(core * half, half), half)
    other = pl.ds(pl.multiple_of((1 - core) * half, half), half)

    query_twin = send(queries_ref.at[other], qbuf.at[z, x, core], twin)
    keys_beside = send(keys_ref, kbuf.at[block(2)], beside)
    pbuf[0] = jnp.broadcast_to(prior_ref[...].astype(jnp.float32), (8, rows))
    prior_beside = send(pbuf.at[0], pbuf.at[2], beside)
    keys_twin = send(keys_ref, kbuf.at[block(1)], twin)
    prior_twin = send(pbuf.at[0], pbuf.at[1], twin)
    qbuf[z, x, core] = queries_ref[mine, :]

    assigned = assign_ref[...]
    assigned = jnp.where(core == 0, assigned[:, :half], assigned[:, half:])
    assigned = jnp.broadcast_to(assigned, (clusters, half))
    row = lax.broadcasted_iota(jnp.int32, (clusters, half), 0)
    seen = jnp.zeros((clusters, half), jnp.int32)
    for owner in range(clusters):
        column = jnp.zeros((clusters, half), jnp.int32)
        for step in range(2 * REACH + 1):
            column = jnp.where(
                row == (owner + step - REACH) % clusters, mask_ref[owner, step], column
            )
        seen = jnp.where(assigned == owner, column, seen)
    vbuf[z] = jnp.where(seen > 0, jnp.float32(0.0), jnp.float32(HIDDEN))
    seen_floor = [None] + [send(vbuf.at[z], vbuf.at[z], floor_peer(by)) for by in range(1, floors)]

    query_twin.wait_recv()
    query_floor = [None] + [
        send(qbuf.at[z, x], qbuf.at[z, x], floor_peer(by)) for by in range(1, floors)
    ]
    query_across = [send(qbuf.at[z, x], qbuf.at[z, x], across)]

    lbuf[block(0), :] = jnp.zeros((rows, 4 * padded), lbuf.dtype)
    for quarter in range(4):
        lbuf[block(0), quarter * padded : quarter * padded + part] = labels_ref[
            :, quarter * part : (quarter + 1) * part
        ]
    labels_beside = send(lbuf.at[block(0)], lbuf.at[block(2)], beside)
    labels_twin = send(lbuf.at[block(0)], lbuf.at[block(1)], twin)
    kbuf[block(0), :] = keys_ref[...]

    def home(by):
        return lax.rem(z - by + floors, floors)

    def forward_query(by):
        query_floor[by].wait_recv()
        source = home(by)
        query_across.append(send(qbuf.at[source, x], qbuf.at[source, x], across))

    forward_query(1)
    keys_beside.wait_recv()
    prior_beside.wait_recv()
    keys_relay = send(kbuf.at[block(2)], kbuf.at[block(3)], twin)
    prior_relay = send(pbuf.at[2], pbuf.at[3], twin)
    for by in range(2, floors):
        forward_query(by)
    for copy in (keys_twin, prior_twin, keys_relay, prior_relay):
        copy.wait_recv()

    def score(by):
        source = home(by)
        query_across[by].wait_recv()
        if by > 0:
            seen_floor[by].wait_recv()
        width = qbuf.shape[4]
        scores = jnp.zeros((4 * rows, half), jnp.float32)
        for quarter in range(4):
            scores = scores + lax.dot_general(
                kbuf[:, quarter * width : (quarter + 1) * width],
                qbuf[source, quarter // 2, quarter % 2],
                (((1,), (1,)), ((), ())),
                preferred_element_type=jnp.float32,
            )
        scores = scores * scale
        near = vbuf[source, pl.ds(cluster, 1), :]
        far = vbuf[source, pl.ds(cluster + 1 - 2 * y, 1), :]
        pieces = []
        for index in range(4):
            bias = spread(pbuf[index, 0:1, :], half)
            pieces.append(
                scores[index * rows : (index + 1) * rows] + bias + (near if index < 2 else far)
            )
        scores = jnp.concatenate(pieces, axis=0)
        top = jnp.max(scores, axis=0, keepdims=True)
        weight = jnp.exp(scores - top)
        total = jnp.sum(weight, axis=0, keepdims=True)
        weights[by] = weight.astype(jnp.bfloat16)
        stats_own[by, 0:1, :] = top
        stats_own[by, 1:2, :] = total
        stats_own[by, 2:8, :] = jnp.zeros((6, half), jnp.float32)

    order = list(range(1, floors)) + [0]
    score(0)
    for by in range(1, floors - 1):
        score(by)
    labels_beside.wait_recv()
    labels_relay = send(lbuf.at[block(2)], lbuf.at[block(3)], twin)
    score(floors - 1)
    labels_twin.wait_recv()
    labels_relay.wait_recv()

    numer_across, stats_across = {}, {}
    wide = 2 * padded
    for by in order:
        numer = lax.dot_general(
            weights[by], lbuf[...], (((0,), (0,)), ((), ())), preferred_element_type=jnp.float32
        )
        low, high = numer[:, :wide], numer[:, wide:]
        numer_out[by] = jnp.where(x == 0, high, low).astype(jnp.bfloat16)
        numer_across[by] = send(numer_out.at[by], numer_in.at[by], across)
        stats_across[by] = send(stats_own.at[by], stats_in.at[by], across)
        numer_own[by] = jnp.where(x == 0, low, high)

    numer_home, stats_home = {}, {}
    for by in order:
        stats_across[by].wait_recv()
        numer_across[by].wait_recv()
        top_own, top_in = stats_own[by, 0:1, :], stats_in[by, 0:1, :]
        top = jnp.maximum(top_own, top_in)
        carry_own, carry_in = jnp.exp(top_own - top), jnp.exp(top_in - top)
        total = stats_own[by, 1:2, :] * carry_own + stats_in[by, 1:2, :] * carry_in
        times = wide // half
        merged = numer_own[by] * widen(spread(carry_own, half), times) + numer_in[by].astype(
            jnp.float32
        ) * widen(spread(carry_in, half), times)
        home_stats_out[by, 0:1, :] = top
        home_stats_out[by, 1:2, :] = total
        home_stats_out[by, 2:8, :] = jnp.zeros((6, half), jnp.float32)
        if by > 0:
            home_out[by] = merged.astype(jnp.bfloat16)
            numer_home[by] = send(home_out.at[by], home_in.at[by], floor_peer(floors - by))
            stats_home[by] = send(
                home_stats_out.at[by], home_stats_in.at[by], floor_peer(floors - by)
            )
        else:
            numer_own[0] = merged

    for by in range(1, floors):
        stats_home[by].wait_recv()
    tops = [home_stats_out[0, 0:1, :]] + [home_stats_in[by, 0:1, :] for by in range(1, floors)]
    totals = [home_stats_out[0, 1:2, :]] + [home_stats_in[by, 1:2, :] for by in range(1, floors)]
    top = functools.reduce(jnp.maximum, tops)
    carries = [jnp.exp(t - top) for t in tops]
    total = functools.reduce(jnp.add, [t * c for t, c in zip(totals, carries)])
    shares = [widen(spread(c / total, half), wide // half) for c in carries]
    result = numer_own[0] * shares[0]
    for by in range(1, floors):
        numer_home[by].wait_recv()
        result = result + home_in[by].astype(jnp.float32) * shares[by]
    result = result.astype(jnp.bfloat16)
    low, high = result[:, :padded], result[:, padded:]
    final_out[...] = jnp.where(core == 0, high, low)
    final = send(final_out, final_in, twin)
    out_ref[mine, :] = jnp.where(core == 0, low, high)[:, :part]
    final.wait_recv()
    out_ref[other, :] = final_in[:, :part]
    for copy in started:
        copy.wait_send()


def plane_body(queries, assign, band_mask, keys, labels, prior):
    clusters = lax.axis_size("cluster")
    floors = clusters // 2
    half, width = queries.shape[0] // 2, queries.shape[1]
    rows, depth = keys.shape
    part = labels.shape[1] // 4
    padded = -(-part // 128) * 128
    vmem = pl.BlockSpec(memory_space=pltpu.VMEM)
    bf16, f32 = jnp.bfloat16, jnp.float32
    copies = 20 + 7 * floors
    return pl.pallas_call(
        functools.partial(plane_kernel, temper / math.sqrt(depth)),
        out_shape=jax.ShapeDtypeStruct((2 * half, part), bf16),
        in_specs=[vmem, vmem, pl.BlockSpec(memory_space=pltpu.SMEM), vmem, vmem, vmem],
        out_specs=vmem,
        scratch_shapes=[
            pltpu.VMEM((floors, 2, 2, half, width), bf16),
            pltpu.VMEM((floors, clusters, half), f32),
            pltpu.VMEM((4 * rows, depth), bf16),
            pltpu.VMEM((4 * rows, 4 * padded), bf16),
            pltpu.VMEM((4, 8, rows), f32),
            pltpu.VMEM((floors, 4 * rows, half), bf16),
            pltpu.VMEM((floors, 8, half), f32),
            pltpu.VMEM((floors, half, 2 * padded), f32),
            pltpu.VMEM((floors, half, 2 * padded), bf16),
            pltpu.VMEM((floors, half, 2 * padded), bf16),
            pltpu.VMEM((floors, 8, half), f32),
            pltpu.VMEM((floors, half, 2 * padded), bf16),
            pltpu.VMEM((floors, 8, half), f32),
            pltpu.VMEM((floors, half, 2 * padded), bf16),
            pltpu.VMEM((floors, 8, half), f32),
            pltpu.VMEM((half, padded), bf16),
            pltpu.VMEM((half, padded), bf16),
            pltpu.SemaphoreType.DMA((copies,)),
            pltpu.SemaphoreType.DMA((copies,)),
        ],
        compiler_params=pltpu.CompilerParams(
            collective_id=0, has_side_effects=True, vmem_limit_bytes=40 * 1024 * 1024
        ),
    )(queries, assign.reshape(1, -1), band_mask, keys, labels, prior.reshape(1, -1))


def from_behind(array, axis, by):
    peers = lax.axis_size(axis)
    return lax.ppermute(array, axis, [(i, (i + by) % peers) for i in range(peers)])


def combined_all(part, axis, combine):
    gathered = jax.tree.map(lambda a: lax.all_gather(a, axis), part)

    def take(source):
        return jax.tree.map(lambda a: lax.dynamic_index_in_dim(a, source, 0, False), gathered)

    return lax.fori_loop(
        1, lax.axis_size(axis), lambda source, state: combine(state, take(source)), take(0)
    )


def combine_totals(first, second):
    top_first, sum_first = first
    top_second, sum_second = second
    highest = jnp.maximum(top_first, top_second)
    return (
        highest,
        sum_first * jnp.exp(top_first - highest) + sum_second * jnp.exp(top_second - highest),
    )


def absorb(state, block, query_full, enabled):
    running, total, accum = state
    block_keys, block_labels, block_prior = block
    scale = temper / math.sqrt(query_full.shape[1])
    scores = (
        jnp.einsum("qd,kd->qk", query_full, block_keys, preferred_element_type=jnp.float32) * scale
    )
    scores = scores + block_prior.astype(jnp.float32)[None, :]
    scores = jnp.where(enabled, scores, jnp.float32(-1e30))
    highest = jnp.maximum(running, jnp.max(scores, axis=1))
    carried = jnp.exp(running - highest)
    weight = jnp.exp(scores - highest[:, None])
    total = total * carried + jnp.sum(weight, axis=1)
    accum = accum * carried[:, None] + jnp.dot(
        weight.astype(jnp.bfloat16), block_labels, preferred_element_type=jnp.float32
    )
    return (highest, total, accum)


def body(queries, assign, band_mask, keys, labels, prior):
    clusters = lax.axis_size("cluster")
    cluster_index = lax.axis_index("cluster")
    local_rows = queries.shape[0]
    capacity = 2 * local_rows // clusters
    slots = clusters * capacity
    target = assign[:, 0]
    onehot = (target[:, None] == jnp.arange(clusters, dtype=jnp.int32)[None, :]).astype(jnp.int32)
    before = jnp.cumsum(onehot, axis=0) - onehot
    position = target * capacity + jnp.sum(before * onehot, axis=1)
    outgoing = jnp.zeros((slots, queries.shape[1]), queries.dtype).at[position].set(queries)
    arrived = lax.all_to_all(
        outgoing.reshape(clusters, capacity, queries.shape[1]),
        "cluster",
        split_axis=0,
        concat_axis=0,
        tiled=True,
    )
    query_full = lax.all_gather(
        arrived.reshape(slots, queries.shape[1]), "feat", axis=1, tiled=True
    )
    mask_row = band_mask[cluster_index]
    classes = labels.shape[1]
    state = (
        jnp.full((slots,), -1e30, jnp.float32),
        jnp.zeros((slots,), jnp.float32),
        jnp.zeros((slots, classes), jnp.float32),
    )
    state = absorb(state, (keys, labels, prior), query_full, jnp.bool_(True))

    def visit(current, block, offset):
        enabled = mask_row[REACH + offset] > 0
        return absorb(current, block, query_full, enabled)

    up_keys, up_labels, up_prior = (keys, labels, prior)
    down_keys, down_labels, down_prior = (keys, labels, prior)
    for reach in range(1, REACH + 1):
        up_keys, up_labels, up_prior = from_behind((up_keys, up_labels, up_prior), "cluster", -1)
        state = visit(state, (up_keys, up_labels, up_prior), reach)
        down_keys, down_labels, down_prior = from_behind(
            (down_keys, down_labels, down_prior), "cluster", 1
        )
        state = visit(state, (down_keys, down_labels, down_prior), -reach)
    running, total, accum = state
    highest, grand_total = combined_all((running, total), "feat", combine_totals)
    factor = jnp.exp(running - highest) / grand_total
    shares = lax.psum_scatter(
        (accum * factor[:, None]).astype(jnp.bfloat16), "feat", scatter_dimension=1, tiled=True
    )
    returned = lax.all_to_all(
        shares.reshape(clusters, capacity, shares.shape[1]),
        "cluster",
        split_axis=0,
        concat_axis=0,
        tiled=True,
    )
    return returned.reshape(slots, shares.shape[1])[position]


def solution(mesh):
    in_specs = (
        P("cluster", "feat"),
        P("cluster", None),
        P(),
        P(("cluster", "feat"), None),
        P(("cluster", "feat"), None),
        P(("cluster", "feat")),
    )
    out_specs = P("cluster", "feat")
    planes = mesh.shape["cluster"] == 8 and mesh.shape["feat"] == 4
    return jax.shard_map(plane_body if planes else body, mesh=mesh, in_specs=in_specs, out_specs=out_specs, check_vma=False)
```

```python
import functools
import math

import jax
import jax.numpy as jnp
from jax import lax
from jax.experimental import pallas as pl
from jax.experimental.pallas import tpu as pltpu
from jax.sharding import PartitionSpec as P

REACH = 3
HIDDEN = -1e30
MESH = pl.DeviceIdType.MESH


temper = 2.0


def spread(row, width):
    return jnp.broadcast_to(row, (width, row.shape[1])).T


def plane_kernel(
    scale,
    queries_ref,
    assign_ref,
    mask_ref,
    keys_ref,
    labels_ref,
    prior_ref,
    out_ref,
    qbuf,
    vbuf,
    kbuf,
    lbuf,
    pbuf,
    weights,
    stats_own,
    numer_own,
    numer_out,
    numer_in,
    stats_in,
    home_out,
    home_stats_out,
    home_in,
    home_stats_in,
    final_out,
    final_in,
    send_sem,
    recv_sem,
    home_sem,
):
    cluster = lax.axis_index("cluster")
    feat = lax.axis_index("feat")
    clusters = mask_ref.shape[0]
    floors = clusters // 2
    half = queries_ref.shape[0] // 2
    rows = keys_ref.shape[0]
    part = labels_ref.shape[0] // 4
    padded = lbuf.shape[2] // 2
    z, y = lax.div(cluster, 2), lax.rem(cluster, 2)
    x, core = lax.div(feat, 2), lax.rem(feat, 2)
    twin = (cluster, feat + 1 - 2 * core)
    across = (cluster, feat + 2 - 4 * x)
    beside = (cluster + 1 - 2 * y, feat)
    above, below = (cluster + 2, feat), (cluster - 2, feat)
    MAIN, EXTRA, ACROSS, SEEN, NUMER, STATS = range(6)

    inner = jnp.minimum(z, floors - 1 - z)
    upper = lax.div(z, 2)

    def home_at(step):
        if step == 0:
            return z
        near = step - inner if step == 1 else step + 0 * inner
        return near + upper * (floors - 1 - 2 * near)

    homes = [home_at(step) for step in range(floors)]

    def floor_peer(floor):
        return (2 * floor + y, feat)

    barrier = pltpu.get_barrier_semaphore()
    peers = [twin, across, beside] + [floor_peer(home) for home in homes[1:]]
    for peer in peers:
        pl.semaphore_signal(barrier, inc=1, device_id=peer, device_id_type=MESH)
    pl.semaphore_wait(barrier, len(peers))

    started = []

    def send(src, dst, peer, where=None, only=None):
        index = len(started)
        copy = pltpu.make_async_remote_copy(
            src_ref=src,
            dst_ref=dst,
            send_sem=send_sem.at[index],
            recv_sem=recv_sem.at[index] if where is None else home_sem.at[where[0], where[1]],
            device_id=peer,
            device_id_type=MESH,
        )
        started.append((copy, only))
        if only is None:
            copy.start()
        else:
            pl.when(only)(copy.start)
        return copy

    def arrived(ref, kind, index):
        pltpu.make_async_remote_copy(
            src_ref=ref,
            dst_ref=ref,
            send_sem=send_sem.at[0],
            recv_sem=home_sem.at[kind, index],
            device_id=twin,
            device_id_type=MESH,
        ).wait_recv()

    mine = pl.ds(pl.multiple_of(core * half, half), half)
    other = pl.ds(pl.multiple_of((1 - core) * half, half), half)

    def block(index):
        return pl.ds(index * rows, rows)

    query_twin = send(queries_ref.at[other], qbuf.at[z, x, core], twin)
    keys_beside = send(keys_ref, kbuf.at[block(2)], beside)
    pbuf[0] = jnp.broadcast_to(prior_ref[...].astype(jnp.float32), (8, rows))
    prior_beside = send(pbuf.at[0], pbuf.at[2], beside)
    keys_twin = send(keys_ref, kbuf.at[block(1)], twin)
    prior_twin = send(pbuf.at[0], pbuf.at[1], twin)
    qbuf[z, x, core] = queries_ref[mine, :]

    def pass_on(home, kind, piece):
        send(piece, piece, above, (kind, home), (home <= z) & (z < floors - 1))
        send(piece, piece, below, (kind, home), (home >= z) & (z > 0))

    query_twin.wait_recv()
    pass_on(z, MAIN, qbuf.at[z, x])
    query_across = send(qbuf.at[z, x], qbuf.at[z, x], across)

    lbuf[0] = jnp.zeros(lbuf.shape[1:], lbuf.dtype)
    for quarter in range(4):
        start = (quarter % 2) * padded
        lbuf[0, quarter // 2, start : start + part, :] = labels_ref[
            quarter * part : (quarter + 1) * part, :
        ]
    labels_beside = [send(lbuf.at[0, side], lbuf.at[2, side], beside) for side in (1 - x, x)]
    labels_twin = [send(lbuf.at[0, side], lbuf.at[1, side], twin) for side in (1 - x, x)]

    assigned = assign_ref[...]
    assigned = jnp.where(core == 0, assigned[:, :half], assigned[:, half:])
    assigned = jnp.broadcast_to(assigned, (clusters, half))
    row = lax.broadcasted_iota(jnp.int32, (clusters, half), 0)
    seen = jnp.zeros((clusters, half), jnp.int32)
    for owner in range(clusters):
        column = jnp.zeros((clusters, half), jnp.int32)
        for step in range(2 * REACH + 1):
            column = jnp.where(
                row == (owner + step - REACH) % clusters, mask_ref[owner, step], column
            )
        seen = jnp.where(assigned == owner, column, seen)
    vbuf[z] = jnp.where(seen > 0, jnp.float32(0.0), jnp.float32(HIDDEN))
    for home in homes[1:]:
        send(vbuf.at[z], vbuf.at[z], floor_peer(home), (SEEN, z))
    kbuf[block(0), :] = keys_ref[...]

    def relay(step):
        home = homes[step]
        arrived(qbuf.at[home, x], MAIN, home)
        pass_on(home, MAIN, qbuf.at[home, x])
        send(qbuf.at[home, x, 0], qbuf.at[home, x, 0], across, (ACROSS, home))
        arrived(qbuf.at[home, 1 - x, 1], EXTRA, home)
        pass_on(home, EXTRA, qbuf.at[home, 1 - x, 1])

    def score(step):
        home = homes[step]
        if step > 0:
            arrived(qbuf.at[home, 1 - x, 0], ACROSS, home)
            arrived(vbuf.at[home], SEEN, home)
        width = qbuf.shape[4]
        scores = jnp.zeros((4 * rows, half), jnp.float32)
        for quarter in range(4):
            scores = scores + lax.dot_general(
                kbuf[:, quarter * width : (quarter + 1) * width],
                qbuf[home, quarter // 2, quarter % 2],
                (((1,), (1,)), ((), ())),
                preferred_element_type=jnp.float32,
            )
        scores = scores * scale
        near = vbuf[home, pl.ds(cluster, 1), :]
        far = vbuf[home, pl.ds(cluster + 1 - 2 * y, 1), :]
        pieces = []
        for index in range(4):
            bias = spread(pbuf[index, 0:1, :], half)
            pieces.append(
                scores[index * rows : (index + 1) * rows] + bias + (near if index < 2 else far)
            )
        scores = jnp.concatenate(pieces, axis=0)
        top = jnp.max(scores, axis=0, keepdims=True)
        weight = jnp.exp(scores - top)
        total = jnp.sum(weight, axis=0, keepdims=True)
        weights[step] = weight.astype(jnp.bfloat16)
        stats_own[step, 0:1, :] = top
        stats_own[step, 1:2, :] = total
        stats_own[step, 2:8, :] = jnp.zeros((6, half), jnp.float32)

    def class_sum(step, side):
        blocks = jnp.concatenate([lbuf[index, side] for index in range(4)], axis=1)
        return jnp.dot(blocks, weights[step], preferred_element_type=jnp.float32)

    numer_across, stats_across = {}, {}

    def send_across(step):
        numer_out[step] = class_sum(step, 1 - x).astype(jnp.bfloat16)
        stats_across[step] = send(stats_own.at[step], stats_in.at[step], across)
        numer_across[step] = send(numer_out.at[step], numer_in.at[step], across)

    query_across.wait_recv()
    pass_on(z, EXTRA, qbuf.at[z, 1 - x, 1])
    relay(1)
    keys_beside.wait_recv()
    prior_beside.wait_recv()
    keys_relay = send(kbuf.at[block(2)], kbuf.at[block(3)], twin)
    prior_relay = send(pbuf.at[2], pbuf.at[3], twin)
    relay(2)
    for copy in (keys_twin, prior_twin, keys_relay, prior_relay):
        copy.wait_recv()
    score(0)
    relay(3)
    score(1)
    labels_beside[0].wait_recv()
    labels_relay = [send(lbuf.at[2, 1 - x], lbuf.at[3, 1 - x], twin)]
    score(2)
    labels_twin[0].wait_recv()
    labels_relay[0].wait_recv()
    send_across(1)
    send_across(2)
    labels_beside[1].wait_recv()
    labels_relay.append(send(lbuf.at[2, x], lbuf.at[3, x], twin))
    score(3)
    send_across(3)
    send_across(0)
    labels_twin[1].wait_recv()
    labels_relay[1].wait_recv()

    for step in (1, 2, 3, 0):
        numer_own[step] = class_sum(step, x)
        stats_across[step].wait_recv()
        numer_across[step].wait_recv()
        top_own, top_in = stats_own[step, 0:1, :], stats_in[step, 0:1, :]
        top = jnp.maximum(top_own, top_in)
        carry_own, carry_in = jnp.exp(top_own - top), jnp.exp(top_in - top)
        total = stats_own[step, 1:2, :] * carry_own + stats_in[step, 1:2, :] * carry_in
        merged = numer_own[step] * carry_own + numer_in[step].astype(jnp.float32) * carry_in
        home_stats_out[step, 0:1, :] = top
        home_stats_out[step, 1:2, :] = total
        home_stats_out[step, 2:8, :] = jnp.zeros((6, half), jnp.float32)
        if step > 0:
            home_out[step] = merged.astype(jnp.bfloat16)
            peer = floor_peer(homes[step])
            send(home_stats_out.at[step], home_stats_in.at[z], peer, (STATS, z))
            send(home_out.at[step], home_in.at[z], peer, (NUMER, z))
        else:
            numer_own[0] = merged

    for home in homes[1:]:
        arrived(home_stats_in.at[home], STATS, home)
    tops = [home_stats_out[0, 0:1, :]] + [home_stats_in[home, 0:1, :] for home in homes[1:]]
    totals = [home_stats_out[0, 1:2, :]] + [home_stats_in[home, 1:2, :] for home in homes[1:]]
    top = functools.reduce(jnp.maximum, tops)
    carries = [jnp.exp(t - top) for t in tops]
    total = functools.reduce(jnp.add, [t * c for t, c in zip(totals, carries)])
    result = numer_own[0] * (carries[0] / total)
    for step in range(1, floors):
        home = homes[step]
        arrived(home_in.at[home], NUMER, home)
        result = result + home_in[home].astype(jnp.float32) * (carries[step] / total)
    low, high = result[:padded].T.astype(jnp.bfloat16), result[padded:].T.astype(jnp.bfloat16)
    final_out[...] = jnp.where(core == 0, high, low)
    final = send(final_out, final_in, twin)
    out_ref[mine, :] = jnp.where(core == 0, low, high)[:, :part]
    final.wait_recv()
    out_ref[other, :] = final_in[:, :part]
    for copy, only in started:
        if only is None:
            copy.wait_send()
        else:
            pl.when(only)(copy.wait_send)


def plane_body(queries, assign, band_mask, keys, labels, prior):
    clusters = lax.axis_size("cluster")
    floors = clusters // 2
    half, width = queries.shape[0] // 2, queries.shape[1]
    rows, depth = keys.shape
    part = labels.shape[1] // 4
    padded = -(-part // 128) * 128
    vmem = pl.BlockSpec(memory_space=pltpu.VMEM)
    bf16, f32 = jnp.bfloat16, jnp.float32
    copies = 64
    return pl.pallas_call(
        functools.partial(plane_kernel, temper / math.sqrt(depth)),
        out_shape=jax.ShapeDtypeStruct((2 * half, part), bf16),
        in_specs=[vmem, vmem, pl.BlockSpec(memory_space=pltpu.SMEM), vmem, vmem, vmem],
        out_specs=vmem,
        scratch_shapes=[
            pltpu.VMEM((floors, 2, 2, half, width), bf16),
            pltpu.VMEM((floors, clusters, half), f32),
            pltpu.VMEM((4 * rows, depth), bf16),
            pltpu.VMEM((4, 2, 2 * padded, rows), bf16),
            pltpu.VMEM((4, 8, rows), f32),
            pltpu.VMEM((floors, 4 * rows, half), bf16),
            pltpu.VMEM((floors, 8, half), f32),
            pltpu.VMEM((floors, 2 * padded, half), f32),
            pltpu.VMEM((floors, 2 * padded, half), bf16),
            pltpu.VMEM((floors, 2 * padded, half), bf16),
            pltpu.VMEM((floors, 8, half), f32),
            pltpu.VMEM((floors, 2 * padded, half), bf16),
            pltpu.VMEM((floors, 8, half), f32),
            pltpu.VMEM((floors, 2 * padded, half), bf16),
            pltpu.VMEM((floors, 8, half), f32),
            pltpu.VMEM((half, padded), bf16),
            pltpu.VMEM((half, padded), bf16),
            pltpu.SemaphoreType.DMA((copies,)),
            pltpu.SemaphoreType.DMA((copies,)),
            pltpu.SemaphoreType.DMA((6, floors)),
        ],
        compiler_params=pltpu.CompilerParams(
            collective_id=0, has_side_effects=True, vmem_limit_bytes=40 * 1024 * 1024
        ),
    )(queries, assign.reshape(1, -1), band_mask, keys, labels.T, prior.reshape(1, -1))


def from_behind(array, axis, by):
    peers = lax.axis_size(axis)
    return lax.ppermute(array, axis, [(i, (i + by) % peers) for i in range(peers)])


def combined_all(part, axis, combine):
    gathered = jax.tree.map(lambda a: lax.all_gather(a, axis), part)

    def take(source):
        return jax.tree.map(lambda a: lax.dynamic_index_in_dim(a, source, 0, False), gathered)

    return lax.fori_loop(
        1, lax.axis_size(axis), lambda source, state: combine(state, take(source)), take(0)
    )


def combine_totals(first, second):
    top_first, sum_first = first
    top_second, sum_second = second
    highest = jnp.maximum(top_first, top_second)
    return (
        highest,
        sum_first * jnp.exp(top_first - highest) + sum_second * jnp.exp(top_second - highest),
    )


def absorb(state, block, query_full, enabled):
    running, total, accum = state
    block_keys, block_labels, block_prior = block
    scale = temper / math.sqrt(query_full.shape[1])
    scores = (
        jnp.einsum("qd,kd->qk", query_full, block_keys, preferred_element_type=jnp.float32) * scale
    )
    scores = scores + block_prior.astype(jnp.float32)[None, :]
    scores = jnp.where(enabled, scores, jnp.float32(-1e30))
    highest = jnp.maximum(running, jnp.max(scores, axis=1))
    carried = jnp.exp(running - highest)
    weight = jnp.exp(scores - highest[:, None])
    total = total * carried + jnp.sum(weight, axis=1)
    accum = accum * carried[:, None] + jnp.dot(
        weight.astype(jnp.bfloat16), block_labels, preferred_element_type=jnp.float32
    )
    return (highest, total, accum)


def body(queries, assign, band_mask, keys, labels, prior):
    clusters = lax.axis_size("cluster")
    cluster_index = lax.axis_index("cluster")
    local_rows = queries.shape[0]
    capacity = 2 * local_rows // clusters
    slots = clusters * capacity
    target = assign[:, 0]
    onehot = (target[:, None] == jnp.arange(clusters, dtype=jnp.int32)[None, :]).astype(jnp.int32)
    before = jnp.cumsum(onehot, axis=0) - onehot
    position = target * capacity + jnp.sum(before * onehot, axis=1)
    outgoing = jnp.zeros((slots, queries.shape[1]), queries.dtype).at[position].set(queries)
    arrived = lax.all_to_all(
        outgoing.reshape(clusters, capacity, queries.shape[1]),
        "cluster",
        split_axis=0,
        concat_axis=0,
        tiled=True,
    )
    query_full = lax.all_gather(
        arrived.reshape(slots, queries.shape[1]), "feat", axis=1, tiled=True
    )
    mask_row = band_mask[cluster_index]
    classes = labels.shape[1]
    state = (
        jnp.full((slots,), -1e30, jnp.float32),
        jnp.zeros((slots,), jnp.float32),
        jnp.zeros((slots, classes), jnp.float32),
    )
    state = absorb(state, (keys, labels, prior), query_full, jnp.bool_(True))

    def visit(current, block, offset):
        enabled = mask_row[REACH + offset] > 0
        return absorb(current, block, query_full, enabled)

    up_keys, up_labels, up_prior = (keys, labels, prior)
    down_keys, down_labels, down_prior = (keys, labels, prior)
    for reach in range(1, REACH + 1):
        up_keys, up_labels, up_prior = from_behind((up_keys, up_labels, up_prior), "cluster", -1)
        state = visit(state, (up_keys, up_labels, up_prior), reach)
        down_keys, down_labels, down_prior = from_behind(
            (down_keys, down_labels, down_prior), "cluster", 1
        )
        state = visit(state, (down_keys, down_labels, down_prior), -reach)
    running, total, accum = state
    highest, grand_total = combined_all((running, total), "feat", combine_totals)
    factor = jnp.exp(running - highest) / grand_total
    shares = lax.psum_scatter(
        (accum * factor[:, None]).astype(jnp.bfloat16), "feat", scatter_dimension=1, tiled=True
    )
    returned = lax.all_to_all(
        shares.reshape(clusters, capacity, shares.shape[1]),
        "cluster",
        split_axis=0,
        concat_axis=0,
        tiled=True,
    )
    return returned.reshape(slots, shares.shape[1])[position]


def solution(mesh):
    in_specs = (
        P("cluster", "feat"),
        P("cluster", None),
        P(),
        P(("cluster", "feat"), None),
        P(("cluster", "feat"), None),
        P(("cluster", "feat")),
    )
    out_specs = P("cluster", "feat")
    planes = mesh.shape["cluster"] == 8 and mesh.shape["feat"] == 4
    return jax.shard_map(plane_body if planes else body, mesh=mesh, in_specs=in_specs, out_specs=out_specs, check_vma=False)
```

```python
import functools
import math

import jax
import jax.numpy as jnp
from jax import lax
from jax.experimental import pallas as pl
from jax.experimental.pallas import tpu as pltpu
from jax.sharding import PartitionSpec as P

REACH = 3
HIDDEN = -1e30
MESH = pl.DeviceIdType.MESH


temper = 2.0


def spread(row, width):
    return jnp.broadcast_to(row, (width, row.shape[1])).T


def plane_kernel(
    scale,
    queries_ref,
    assign_ref,
    mask_ref,
    keys_ref,
    labels_ref,
    prior_ref,
    out_ref,
    assign_buf,
    mask_buf,
    prior_buf,
    labels_buf,
    qbuf,
    vbuf,
    kbuf,
    lbuf,
    pbuf,
    bias,
    weights,
    stats_own,
    numer_own,
    numer_out,
    numer_in,
    stats_in,
    home_out,
    home_stats_out,
    home_in,
    home_stats_in,
    send_sem,
    recv_sem,
    home_sem,
    load_sem,
):
    cluster = lax.axis_index("cluster")
    feat = lax.axis_index("feat")
    clusters = mask_ref.shape[0]
    floors = clusters // 2
    half = queries_ref.shape[0] // 2
    rows = keys_ref.shape[0]
    part = labels_ref.shape[0] // 4
    padded = lbuf.shape[2] // 2
    z, y = lax.div(cluster, 2), lax.rem(cluster, 2)
    x, core = lax.div(feat, 2), lax.rem(feat, 2)
    twin = (cluster, feat + 1 - 2 * core)
    across = (cluster, feat + 2 - 4 * x)
    beside = (cluster + 1 - 2 * y, feat)

    def mate(peer):
        return (peer[0], peer[1] + 1 - 2 * core)

    above, below = (cluster + 2, feat), (cluster - 2, feat)
    FIRST, SECOND, EXTRA, ACROSS, SEEN, NUMER, STATS = range(7)

    loads = [
        pltpu.make_async_copy(src, dst, load_sem.at[index])
        for index, (src, dst) in enumerate(
            [
                (queries_ref.at[pl.ds(core * half, half)], qbuf.at[z, x, core]),
                (prior_ref, prior_buf),
                (labels_ref, labels_buf),
                (mask_ref, mask_buf),
                (assign_ref, assign_buf),
                (keys_ref, kbuf.at[pl.ds(0, rows)]),
            ]
        )
    ]
    for load in loads:
        load.start()

    inner = jnp.minimum(z, floors - 1 - z)
    upper = lax.div(z, 2)

    def home_at(step):
        if step == 0:
            return z
        near = step - inner if step == 1 else step + 0 * inner
        return near + upper * (floors - 1 - 2 * near)

    homes = [home_at(step) for step in range(floors)]

    def floor_peer(floor):
        return (2 * floor + y, feat)

    barrier = pltpu.get_barrier_semaphore()
    peers = [twin, across, mate(across), beside]
    for home in homes[1:]:
        peers += [floor_peer(home), mate(floor_peer(home))]
    for peer in peers:
        pl.semaphore_signal(barrier, inc=1, device_id=peer, device_id_type=MESH)
    pl.semaphore_wait(barrier, len(peers))

    started = []

    def send(src, dst, peer, where=None, only=None):
        index = len(started)
        copy = pltpu.make_async_remote_copy(
            src_ref=src,
            dst_ref=dst,
            send_sem=send_sem.at[index],
            recv_sem=recv_sem.at[index] if where is None else home_sem.at[where[0], where[1]],
            device_id=peer,
            device_id_type=MESH,
        )
        started.append((copy, only))
        if only is None:
            copy.start()
        else:
            pl.when(only)(copy.start)
        return copy

    def arrived(ref, kind, index):
        pltpu.make_async_remote_copy(
            src_ref=ref,
            dst_ref=ref,
            send_sem=send_sem.at[0],
            recv_sem=home_sem.at[kind, index],
            device_id=twin,
            device_id_type=MESH,
        ).wait_recv()

    mine = pl.ds(pl.multiple_of(core * half, half), half)
    other = pl.ds(pl.multiple_of((1 - core) * half, half), half)
    up, down = z < floors - 1, z > 0

    def block(index):
        return pl.ds(index * rows, rows)

    own, piece = qbuf.at[z, x, core], core
    query_twin = send(queries_ref.at[other], own, twin)
    send(queries_ref.at[mine], own, above, (FIRST + piece, z), up)
    send(queries_ref.at[mine], own, below, (FIRST + piece, z), down)
    send(queries_ref.at[other], own, mate(above), (FIRST + piece, z), up)
    send(queries_ref.at[other], own, mate(below), (FIRST + piece, z), down)
    send(queries_ref.at[mine], own, across, (FIRST + piece, z))
    send(queries_ref.at[other], own, mate(across), (FIRST + piece, z))
    keys_beside = send(keys_ref, kbuf.at[block(2)], beside)
    keys_twin = send(keys_ref, kbuf.at[block(1)], twin)
    loads[1].wait()
    pbuf[0] = jnp.broadcast_to(prior_buf[...].astype(jnp.float32), (8, rows))
    prior_beside = send(pbuf.at[0], pbuf.at[2], beside)
    prior_twin = send(pbuf.at[0], pbuf.at[1], twin)

    def pass_on(home, kind, ref, start=False):
        send(ref, ref, above, (kind, home), (home <= z if start else home < z) & up)
        send(ref, ref, below, (kind, home), (home >= z if start else home > z) & down)

    lbuf[0] = jnp.zeros(lbuf.shape[1:], lbuf.dtype)
    loads[2].wait()
    for quarter in range(4):
        start = (quarter % 2) * padded
        lbuf[0, quarter // 2, start : start + part, :] = labels_buf[
            quarter * part : (quarter + 1) * part, :
        ]
    labels_beside = [send(lbuf.at[0, side], lbuf.at[2, side], beside) for side in (1 - x, x)]
    labels_twin = [send(lbuf.at[0, side], lbuf.at[1, side], twin) for side in (1 - x, x)]

    loads[3].wait()
    loads[4].wait()
    assigned = assign_buf[...]
    assigned = jnp.where(core == 0, assigned[:, :half], assigned[:, half:])
    assigned = jnp.broadcast_to(assigned, (clusters, half))
    row = lax.broadcasted_iota(jnp.int32, (clusters, half), 0)
    seen = jnp.zeros((clusters, half), jnp.int32)
    for owner in range(clusters):
        column = jnp.zeros((clusters, half), jnp.int32)
        for step in range(2 * REACH + 1):
            column = jnp.where(
                row == (owner + step - REACH) % clusters, mask_buf[owner, step], column
            )
        seen = jnp.where(assigned == owner, column, seen)
    vbuf[z] = jnp.where(seen > 0, jnp.float32(0.0), jnp.float32(HIDDEN))
    for home in homes[1:]:
        send(vbuf.at[z], vbuf.at[z], floor_peer(home), (SEEN, z))

    def relay(step):
        home = homes[step]
        first, second, extra = qbuf.at[home, x, 0], qbuf.at[home, x, 1], qbuf.at[home, 1 - x, 1]
        arrived(first, FIRST, home)
        pass_on(home, FIRST, first)
        send(first, first, across, (ACROSS, home))
        arrived(second, SECOND, home)
        pass_on(home, SECOND, second)
        arrived(extra, EXTRA, home)
        pass_on(home, EXTRA, extra)

    def score(step):
        home = homes[step]
        if step > 0:
            arrived(qbuf.at[home, 1 - x, 0], ACROSS, home)
            arrived(vbuf.at[home], SEEN, home)
        width = qbuf.shape[4]
        scores = jnp.zeros((4 * rows, half), jnp.float32)
        for quarter in range(4):
            scores = scores + lax.dot_general(
                kbuf[:, quarter * width : (quarter + 1) * width],
                qbuf[home, quarter // 2, quarter % 2],
                (((1,), (1,)), ((), ())),
                preferred_element_type=jnp.float32,
            )
        scores = scores * scale
        near = vbuf[home, pl.ds(cluster, 1), :]
        far = vbuf[home, pl.ds(cluster + 1 - 2 * y, 1), :]
        pieces = []
        for index in range(4):
            cut = slice(index * rows, (index + 1) * rows)
            pieces.append(scores[cut] + bias[cut, :] + (near if index < 2 else far))
        scores = jnp.concatenate(pieces, axis=0)
        top = jnp.max(scores, axis=0, keepdims=True)
        weight = jnp.exp(scores - top)
        total = jnp.sum(weight, axis=0, keepdims=True)
        weights[step] = weight.astype(jnp.bfloat16)
        stats_own[step, 0:1, :] = top
        stats_own[step, 1:2, :] = total
        stats_own[step, 2:8, :] = jnp.zeros((6, half), jnp.float32)

    def class_sum(step, side):
        blocks = jnp.concatenate([lbuf[index, side] for index in range(4)], axis=1)
        return jnp.dot(blocks, weights[step], preferred_element_type=jnp.float32)

    numer_across, stats_across = {}, {}

    def send_across(step):
        numer_out[step] = class_sum(step, 1 - x).astype(jnp.bfloat16)
        stats_across[step] = send(stats_own.at[step], stats_in.at[step], across)
        numer_across[step] = send(numer_out.at[step], numer_in.at[step], across)

    arrived(qbuf.at[z, 1 - x, 0], FIRST, z)
    arrived(qbuf.at[z, 1 - x, 1], SECOND, z)
    pass_on(z, EXTRA, qbuf.at[z, 1 - x, 1], True)
    relay(1)
    keys_beside.wait_recv()
    prior_beside.wait_recv()
    keys_relay = send(kbuf.at[block(2)], kbuf.at[block(3)], twin)
    prior_relay = send(pbuf.at[2], pbuf.at[3], twin)
    relay(2)
    for copy in (keys_twin, prior_twin, keys_relay, prior_relay, query_twin):
        copy.wait_recv()
    loads[0].wait()
    loads[5].wait()
    for index in range(4):
        bias[block(index), :] = spread(pbuf[index, 0:1, :], half)
    score(0)
    relay(3)
    score(1)
    labels_beside[0].wait_recv()
    labels_relay = [send(lbuf.at[2, 1 - x], lbuf.at[3, 1 - x], twin)]
    score(2)
    labels_twin[0].wait_recv()
    labels_relay[0].wait_recv()
    send_across(1)
    send_across(2)
    labels_beside[1].wait_recv()
    labels_relay.append(send(lbuf.at[2, x], lbuf.at[3, x], twin))
    score(3)
    send_across(3)
    send_across(0)
    labels_twin[1].wait_recv()
    labels_relay[1].wait_recv()

    for step in (1, 2, 3, 0):
        numer_own[step] = class_sum(step, x)
        stats_across[step].wait_recv()
        numer_across[step].wait_recv()
        top_own, top_in = stats_own[step, 0:1, :], stats_in[step, 0:1, :]
        top = jnp.maximum(top_own, top_in)
        carry_own, carry_in = jnp.exp(top_own - top), jnp.exp(top_in - top)
        total = stats_own[step, 1:2, :] * carry_own + stats_in[step, 1:2, :] * carry_in
        merged = numer_own[step] * carry_own + numer_in[step].astype(jnp.float32) * carry_in
        home_stats_out[step, 0:1, :] = top
        home_stats_out[step, 1:2, :] = total
        home_stats_out[step, 2:8, :] = jnp.zeros((6, half), jnp.float32)
        home_out[step, 0] = merged[:padded].astype(jnp.bfloat16)
        home_out[step, 1] = merged[padded:].astype(jnp.bfloat16)
        place = 2 * z + core
        peer = floor_peer(homes[step])
        if step > 0:
            send(home_stats_out.at[step], home_stats_in.at[place], peer, (STATS, place))
            send(home_out.at[step, core], home_in.at[place], peer, (NUMER, place))
        else:
            home_stats_in[place] = home_stats_out[0]
            home_in[place] = home_out[0, core]
        send(home_stats_out.at[step], home_stats_in.at[place], mate(peer), (STATS, place))
        send(home_out.at[step, 1 - core], home_in.at[place], mate(peer), (NUMER, place))

    for side in (0, 1):
        source = core if side == 0 else 1 - core
        places = [2 * home + source for home in homes]
        for step in range(floors):
            if side + step > 0:
                arrived(home_stats_in.at[places[step]], STATS, places[step])
        tops = [home_stats_in[place, 0:1, :] for place in places]
        totals = [home_stats_in[place, 1:2, :] for place in places]
        top = functools.reduce(jnp.maximum, tops)
        carries = [jnp.exp(t - top) for t in tops]
        total = functools.reduce(jnp.add, [t * c for t, c in zip(totals, carries)])
        result = jnp.zeros((padded, half), jnp.float32)
        for step in range(floors):
            if side + step > 0:
                arrived(home_in.at[places[step]], NUMER, places[step])
            result = result + home_in[places[step]].astype(jnp.float32) * (carries[step] / total)
        out_ref[mine if side == 0 else other, :] = result.T.astype(jnp.bfloat16)[:, :part]
    for copy, only in started:
        if only is None:
            copy.wait_send()
        else:
            pl.when(only)(copy.wait_send)


def plane_body(queries, assign, band_mask, keys, labels, prior):
    clusters = lax.axis_size("cluster")
    floors = clusters // 2
    half, width = queries.shape[0] // 2, queries.shape[1]
    rows, depth = keys.shape
    part = labels.shape[1] // 4
    padded = -(-part // 128) * 128
    vmem = pl.BlockSpec(memory_space=pltpu.VMEM)
    bf16, f32 = jnp.bfloat16, jnp.float32
    copies = 80
    return pl.pallas_call(
        functools.partial(plane_kernel, temper / math.sqrt(depth)),
        out_shape=jax.ShapeDtypeStruct((2 * half, part), bf16),
        in_specs=[pl.BlockSpec(memory_space=pltpu.HBM)] * 6,
        out_specs=vmem,
        scratch_shapes=[
            pltpu.VMEM((1, 2 * half), jnp.int32),
            pltpu.SMEM(band_mask.shape, jnp.int32),
            pltpu.VMEM((1, rows), bf16),
            pltpu.VMEM((4 * part, rows), bf16),
            pltpu.VMEM((floors, 2, 2, half, width), bf16),
            pltpu.VMEM((floors, clusters, half), f32),
            pltpu.VMEM((4 * rows, depth), bf16),
            pltpu.VMEM((4, 2, 2 * padded, rows), bf16),
            pltpu.VMEM((4, 8, rows), f32),
            pltpu.VMEM((4 * rows, half), f32),
            pltpu.VMEM((floors, 4 * rows, half), bf16),
            pltpu.VMEM((floors, 8, half), f32),
            pltpu.VMEM((floors, 2 * padded, half), f32),
            pltpu.VMEM((floors, 2 * padded, half), bf16),
            pltpu.VMEM((floors, 2 * padded, half), bf16),
            pltpu.VMEM((floors, 8, half), f32),
            pltpu.VMEM((floors, 2, padded, half), bf16),
            pltpu.VMEM((floors, 8, half), f32),
            pltpu.VMEM((2 * floors, padded, half), bf16),
            pltpu.VMEM((2 * floors, 8, half), f32),
            pltpu.SemaphoreType.DMA((copies,)),
            pltpu.SemaphoreType.DMA((copies,)),
            pltpu.SemaphoreType.DMA((7, 2 * floors)),
            pltpu.SemaphoreType.DMA((6,)),
        ],
        compiler_params=pltpu.CompilerParams(
            collective_id=0, has_side_effects=True, vmem_limit_bytes=60 * 1024 * 1024
        ),
    )(queries, assign.reshape(1, -1), band_mask, keys, labels.T, prior.reshape(1, -1))


def from_behind(array, axis, by):
    peers = lax.axis_size(axis)
    return lax.ppermute(array, axis, [(i, (i + by) % peers) for i in range(peers)])


def combined_all(part, axis, combine):
    gathered = jax.tree.map(lambda a: lax.all_gather(a, axis), part)

    def take(source):
        return jax.tree.map(lambda a: lax.dynamic_index_in_dim(a, source, 0, False), gathered)

    return lax.fori_loop(
        1, lax.axis_size(axis), lambda source, state: combine(state, take(source)), take(0)
    )


def combine_totals(first, second):
    top_first, sum_first = first
    top_second, sum_second = second
    highest = jnp.maximum(top_first, top_second)
    return (
        highest,
        sum_first * jnp.exp(top_first - highest) + sum_second * jnp.exp(top_second - highest),
    )


def absorb(state, block, query_full, enabled):
    running, total, accum = state
    block_keys, block_labels, block_prior = block
    scale = temper / math.sqrt(query_full.shape[1])
    scores = (
        jnp.einsum("qd,kd->qk", query_full, block_keys, preferred_element_type=jnp.float32) * scale
    )
    scores = scores + block_prior.astype(jnp.float32)[None, :]
    scores = jnp.where(enabled, scores, jnp.float32(-1e30))
    highest = jnp.maximum(running, jnp.max(scores, axis=1))
    carried = jnp.exp(running - highest)
    weight = jnp.exp(scores - highest[:, None])
    total = total * carried + jnp.sum(weight, axis=1)
    accum = accum * carried[:, None] + jnp.dot(
        weight.astype(jnp.bfloat16), block_labels, preferred_element_type=jnp.float32
    )
    return (highest, total, accum)


def body(queries, assign, band_mask, keys, labels, prior):
    clusters = lax.axis_size("cluster")
    cluster_index = lax.axis_index("cluster")
    local_rows = queries.shape[0]
    capacity = 2 * local_rows // clusters
    slots = clusters * capacity
    target = assign[:, 0]
    onehot = (target[:, None] == jnp.arange(clusters, dtype=jnp.int32)[None, :]).astype(jnp.int32)
    before = jnp.cumsum(onehot, axis=0) - onehot
    position = target * capacity + jnp.sum(before * onehot, axis=1)
    outgoing = jnp.zeros((slots, queries.shape[1]), queries.dtype).at[position].set(queries)
    arrived = lax.all_to_all(
        outgoing.reshape(clusters, capacity, queries.shape[1]),
        "cluster",
        split_axis=0,
        concat_axis=0,
        tiled=True,
    )
    query_full = lax.all_gather(
        arrived.reshape(slots, queries.shape[1]), "feat", axis=1, tiled=True
    )
    mask_row = band_mask[cluster_index]
    classes = labels.shape[1]
    state = (
        jnp.full((slots,), -1e30, jnp.float32),
        jnp.zeros((slots,), jnp.float32),
        jnp.zeros((slots, classes), jnp.float32),
    )
    state = absorb(state, (keys, labels, prior), query_full, jnp.bool_(True))

    def visit(current, block, offset):
        enabled = mask_row[REACH + offset] > 0
        return absorb(current, block, query_full, enabled)

    up_keys, up_labels, up_prior = (keys, labels, prior)
    down_keys, down_labels, down_prior = (keys, labels, prior)
    for reach in range(1, REACH + 1):
        up_keys, up_labels, up_prior = from_behind((up_keys, up_labels, up_prior), "cluster", -1)
        state = visit(state, (up_keys, up_labels, up_prior), reach)
        down_keys, down_labels, down_prior = from_behind(
            (down_keys, down_labels, down_prior), "cluster", 1
        )
        state = visit(state, (down_keys, down_labels, down_prior), -reach)
    running, total, accum = state
    highest, grand_total = combined_all((running, total), "feat", combine_totals)
    factor = jnp.exp(running - highest) / grand_total
    shares = lax.psum_scatter(
        (accum * factor[:, None]).astype(jnp.bfloat16), "feat", scatter_dimension=1, tiled=True
    )
    returned = lax.all_to_all(
        shares.reshape(clusters, capacity, shares.shape[1]),
        "cluster",
        split_axis=0,
        concat_axis=0,
        tiled=True,
    )
    return returned.reshape(slots, shares.shape[1])[position]


def solution(mesh):
    in_specs = (
        P("cluster", "feat"),
        P("cluster", None),
        P(),
        P(("cluster", "feat"), None),
        P(("cluster", "feat"), None),
        P(("cluster", "feat")),
    )
    out_specs = P("cluster", "feat")
    planes = mesh.shape["cluster"] == 8 and mesh.shape["feat"] == 4
    return jax.shard_map(plane_body if planes else body, mesh=mesh, in_specs=in_specs, out_specs=out_specs, check_vma=False)
```

```python
import functools
import math

import jax
import jax.numpy as jnp
from jax import lax
from jax.experimental import pallas as pl
from jax.experimental.pallas import tpu as pltpu
from jax.sharding import PartitionSpec as P

REACH = 3
HIDDEN = -1e30
MESH = pl.DeviceIdType.MESH


temper = 2.0


def spread(row, width):
    return jnp.broadcast_to(row, (width, row.shape[1])).T


def plane_kernel(
    scale,
    queries_ref,
    assign_ref,
    mask_ref,
    keys_ref,
    labels_ref,
    prior_ref,
    out_ref,
    assign_buf,
    mask_buf,
    prior_buf,
    labels_buf,
    qbuf,
    vbuf,
    kbuf,
    lbuf,
    pbuf,
    bias,
    weights,
    stats_own,
    numer_out,
    numer_in,
    stats_in,
    home_out,
    home_stats_out,
    home_in,
    home_stats_in,
    send_sem,
    recv_sem,
    home_sem,
    load_sem,
):
    cluster = lax.axis_index("cluster")
    feat = lax.axis_index("feat")
    clusters = mask_ref.shape[0]
    floors = clusters // 2
    half = queries_ref.shape[0] // 2
    rows = keys_ref.shape[0]
    part = labels_ref.shape[0] // 4
    padded = lbuf.shape[3]
    z, y = lax.div(cluster, 2), lax.rem(cluster, 2)
    x, core = lax.div(feat, 2), lax.rem(feat, 2)
    twin = (cluster, feat + 1 - 2 * core)
    across = (cluster, feat + 2 - 4 * x)
    beside = (cluster + 1 - 2 * y, feat)

    def mate(peer):
        return (peer[0], peer[1] + 1 - 2 * core)

    above, below = (cluster + 2, feat), (cluster - 2, feat)
    FIRST, SECOND, EXTRA, ACROSS, SEEN, NUMER, STATS = range(7)

    loads = [
        pltpu.make_async_copy(src, dst, load_sem.at[index])
        for index, (src, dst) in enumerate(
            [
                (queries_ref.at[pl.ds(core * half, half)], qbuf.at[z, x, core]),
                (prior_ref, prior_buf),
                (labels_ref, labels_buf),
                (mask_ref, mask_buf),
                (assign_ref, assign_buf),
                (keys_ref, kbuf.at[pl.ds(0, rows)]),
            ]
        )
    ]
    for load in loads:
        load.start()

    inner = jnp.minimum(z, floors - 1 - z)
    upper = lax.div(z, 2)

    def home_at(step):
        if step == 0:
            return z
        near = step - inner if step == 1 else step + 0 * inner
        return near + upper * (floors - 1 - 2 * near)

    homes = [home_at(step) for step in range(floors)]

    def floor_peer(floor):
        return (2 * floor + y, feat)

    barrier = pltpu.get_barrier_semaphore()
    peers = [twin, across, mate(across), beside]
    for home in homes[1:]:
        peers += [floor_peer(home), mate(floor_peer(home))]
    for peer in peers:
        pl.semaphore_signal(barrier, inc=1, device_id=peer, device_id_type=MESH)
    pl.semaphore_wait(barrier, len(peers))

    started = []

    def send(src, dst, peer, where=None, only=None):
        index = len(started)
        copy = pltpu.make_async_remote_copy(
            src_ref=src,
            dst_ref=dst,
            send_sem=send_sem.at[index],
            recv_sem=recv_sem.at[index] if where is None else home_sem.at[where[0], where[1]],
            device_id=peer,
            device_id_type=MESH,
        )
        started.append((copy, only))
        if only is None:
            copy.start()
        else:
            pl.when(only)(copy.start)
        return copy

    def arrived(ref, kind, index):
        pltpu.make_async_remote_copy(
            src_ref=ref,
            dst_ref=ref,
            send_sem=send_sem.at[0],
            recv_sem=home_sem.at[kind, index],
            device_id=twin,
            device_id_type=MESH,
        ).wait_recv()

    mine = pl.ds(pl.multiple_of(core * half, half), half)
    other = pl.ds(pl.multiple_of((1 - core) * half, half), half)
    up, down = z < floors - 1, z > 0

    def block(index):
        return pl.ds(index * rows, rows)

    own, piece = qbuf.at[z, x, core], core
    query_twin = send(queries_ref.at[other], own, twin)
    send(queries_ref.at[mine], own, above, (FIRST + piece, z), up)
    send(queries_ref.at[mine], own, below, (FIRST + piece, z), down)
    send(queries_ref.at[other], own, mate(above), (FIRST + piece, z), up)
    send(queries_ref.at[other], own, mate(below), (FIRST + piece, z), down)
    send(queries_ref.at[mine], own, across, (FIRST + piece, z))
    send(queries_ref.at[other], own, mate(across), (FIRST + piece, z))
    keys_beside = send(keys_ref, kbuf.at[block(2)], beside)
    keys_twin = send(keys_ref, kbuf.at[block(1)], twin)
    loads[1].wait()
    pbuf[0] = jnp.broadcast_to(prior_buf[...].astype(jnp.float32), (8, rows))
    prior_beside = send(pbuf.at[0], pbuf.at[2], beside)
    prior_twin = send(pbuf.at[0], pbuf.at[1], twin)

    def pass_on(home, kind, ref, start=False):
        send(ref, ref, above, (kind, home), (home <= z if start else home < z) & up)
        send(ref, ref, below, (kind, home), (home >= z if start else home > z) & down)

    lbuf[0] = jnp.zeros(lbuf.shape[1:], lbuf.dtype)
    loads[2].wait()
    for quarter in range(4):
        lbuf[0, quarter // 2, quarter % 2, :part, :] = labels_buf[
            quarter * part : (quarter + 1) * part, :
        ]
    quarters = [(1 - x, 0), (1 - x, 1), (x, 0), (x, 1)]
    labels_beside, labels_twin, labels_relay = [], [], []
    for side, turn in quarters:
        labels_beside.append(send(lbuf.at[0, side, turn], lbuf.at[2, side, turn], beside))
        labels_twin.append(send(lbuf.at[0, side, turn], lbuf.at[1, side, turn], twin))

    def relay_labels(index):
        side, turn = quarters[index]
        labels_beside[index].wait_recv()
        labels_relay.append(send(lbuf.at[2, side, turn], lbuf.at[3, side, turn], twin))

    def labels_here(index):
        labels_twin[index].wait_recv()
        labels_relay[index].wait_recv()

    loads[3].wait()
    loads[4].wait()
    assigned = assign_buf[...]
    assigned = jnp.where(core == 0, assigned[:, :half], assigned[:, half:])
    assigned = jnp.broadcast_to(assigned, (clusters, half))
    row = lax.broadcasted_iota(jnp.int32, (clusters, half), 0)
    seen = jnp.zeros((clusters, half), jnp.int32)
    for owner in range(clusters):
        column = jnp.zeros((clusters, half), jnp.int32)
        for step in range(2 * REACH + 1):
            column = jnp.where(
                row == (owner + step - REACH) % clusters, mask_buf[owner, step], column
            )
        seen = jnp.where(assigned == owner, column, seen)
    vbuf[z] = jnp.where(seen > 0, jnp.float32(0.0), jnp.float32(HIDDEN))
    for home in homes[1:]:
        send(vbuf.at[z], vbuf.at[z], floor_peer(home), (SEEN, z))

    def relay(step):
        home = homes[step]
        first, second, extra = qbuf.at[home, x, 0], qbuf.at[home, x, 1], qbuf.at[home, 1 - x, 1]
        arrived(first, FIRST, home)
        pass_on(home, FIRST, first)
        send(first, first, across, (ACROSS, home))
        arrived(second, SECOND, home)
        pass_on(home, SECOND, second)
        arrived(extra, EXTRA, home)
        pass_on(home, EXTRA, extra)

    def score(step):
        home = homes[step]
        if step > 0:
            arrived(qbuf.at[home, 1 - x, 0], ACROSS, home)
            arrived(vbuf.at[home], SEEN, home)
        width = qbuf.shape[4]
        scores = jnp.zeros((4 * rows, half), jnp.float32)
        for quarter in range(4):
            scores = scores + lax.dot_general(
                kbuf[:, quarter * width : (quarter + 1) * width],
                qbuf[home, quarter // 2, quarter % 2],
                (((1,), (1,)), ((), ())),
                preferred_element_type=jnp.float32,
            )
        scores = scores * scale
        near = vbuf[home, pl.ds(cluster, 1), :]
        far = vbuf[home, pl.ds(cluster + 1 - 2 * y, 1), :]
        pieces = []
        for index in range(4):
            cut = slice(index * rows, (index + 1) * rows)
            pieces.append(scores[cut] + bias[cut, :] + (near if index < 2 else far))
        scores = jnp.concatenate(pieces, axis=0)
        top = jnp.max(scores, axis=0, keepdims=True)
        weight = jnp.exp(scores - top)
        total = jnp.sum(weight, axis=0, keepdims=True)
        weights[step] = weight.astype(jnp.bfloat16)
        stats_own[step, 0:1, :] = top
        stats_own[step, 1:2, :] = total
        stats_own[step, 2:8, :] = jnp.zeros((6, half), jnp.float32)

    def class_sum(step, side, turn):
        blocks = jnp.concatenate([lbuf[index, side, turn] for index in range(4)], axis=1)
        return jnp.dot(blocks, weights[step], preferred_element_type=jnp.float32)

    numer_across, stats_across, carried = {}, {}, {}

    def send_across(step, turn):
        numer_out[step, turn] = class_sum(step, 1 - x, turn).astype(jnp.bfloat16)
        if turn == 0:
            stats_across[step] = send(stats_own.at[step], stats_in.at[step], across)
        numer_across[step, turn] = send(
            numer_out.at[step, turn], numer_in.at[step, turn], across
        )

    place = 2 * z + core

    def merge(step, turn):
        numer = class_sum(step, x, turn)
        floor = homes[step]
        if turn == 0:
            stats_across[step].wait_recv()
            top_own, top_in = stats_own[step, 0:1, :], stats_in[step, 0:1, :]
            top = jnp.maximum(top_own, top_in)
            carry_own, carry_in = jnp.exp(top_own - top), jnp.exp(top_in - top)
            total = stats_own[step, 1:2, :] * carry_own + stats_in[step, 1:2, :] * carry_in
            carried[step] = carry_own, carry_in
            home_stats_out[step, 0:1, :] = top
            home_stats_out[step, 1:2, :] = total
            home_stats_out[step, 2:8, :] = jnp.zeros((6, half), jnp.float32)
            if step > 0:
                for peer in (floor_peer(floor), mate(floor_peer(floor))):
                    send(home_stats_out.at[step], home_stats_in.at[place], peer, (STATS, place))
            else:
                home_stats_in[place] = home_stats_out[0]
                send(home_stats_out.at[0], home_stats_in.at[place], twin, (STATS, place))
        carry_own, carry_in = carried[step]
        numer_across[step, turn].wait_recv()
        merged = numer * carry_own + numer_in[step, turn].astype(jnp.float32) * carry_in
        home_out[step, turn] = merged.astype(jnp.bfloat16)
        if step > 0:
            peer = (2 * floor + y, 2 * x + turn)
            send(home_out.at[step, turn], home_in.at[place], peer, (NUMER, place))
        elif turn == 1:
            home_in[place] = home_out[0, core]
            send(home_out.at[0, 1 - core], home_in.at[place], twin, (NUMER, place))

    arrived(qbuf.at[z, 1 - x, 0], FIRST, z)
    arrived(qbuf.at[z, 1 - x, 1], SECOND, z)
    pass_on(z, EXTRA, qbuf.at[z, 1 - x, 1], True)
    relay(1)
    keys_beside.wait_recv()
    prior_beside.wait_recv()
    keys_relay = send(kbuf.at[block(2)], kbuf.at[block(3)], twin)
    prior_relay = send(pbuf.at[2], pbuf.at[3], twin)
    relay(2)
    for copy in (keys_twin, prior_twin, keys_relay, prior_relay, query_twin):
        copy.wait_recv()
    loads[0].wait()
    loads[5].wait()
    for index in range(4):
        bias[block(index), :] = spread(pbuf[index, 0:1, :], half)
    score(0)
    score(1)
    relay_labels(0)
    score(2)
    relay(3)
    labels_here(0)
    send_across(2, 0)
    relay_labels(1)
    score(3)
    labels_here(1)
    send_across(2, 1)
    send_across(3, 0)
    send_across(3, 1)
    relay_labels(2)
    send_across(1, 0)
    send_across(1, 1)
    labels_here(2)
    merge(2, 0)
    relay_labels(3)
    labels_here(3)
    merge(2, 1)
    merge(3, 0)
    send_across(0, 0)
    send_across(0, 1)
    merge(3, 1)
    for step in (1, 0):
        merge(step, 0)
        merge(step, 1)

    for side in (0, 1):
        source = core if side == 0 else 1 - core
        places = [2 * home + source for home in homes]
        for step in range(floors):
            if side + step > 0:
                arrived(home_stats_in.at[places[step]], STATS, places[step])
        tops = [home_stats_in[place, 0:1, :] for place in places]
        totals = [home_stats_in[place, 1:2, :] for place in places]
        top = functools.reduce(jnp.maximum, tops)
        carries = [jnp.exp(t - top) for t in tops]
        total = functools.reduce(jnp.add, [t * c for t, c in zip(totals, carries)])
        result = jnp.zeros((padded, half), jnp.float32)
        for step in range(floors):
            if side + step > 0:
                arrived(home_in.at[places[step]], NUMER, places[step])
            result = result + home_in[places[step]].astype(jnp.float32) * (carries[step] / total)
        out_ref[mine if side == 0 else other, :] = result.T.astype(jnp.bfloat16)[:, :part]
    for copy, only in started:
        if only is None:
            copy.wait_send()
        else:
            pl.when(only)(copy.wait_send)


def plane_body(queries, assign, band_mask, keys, labels, prior):
    clusters = lax.axis_size("cluster")
    floors = clusters // 2
    half, width = queries.shape[0] // 2, queries.shape[1]
    rows, depth = keys.shape
    part = labels.shape[1] // 4
    padded = -(-part // 128) * 128
    vmem = pl.BlockSpec(memory_space=pltpu.VMEM)
    bf16, f32 = jnp.bfloat16, jnp.float32
    copies = 96
    return pl.pallas_call(
        functools.partial(plane_kernel, temper / math.sqrt(depth)),
        out_shape=jax.ShapeDtypeStruct((2 * half, part), bf16),
        in_specs=[pl.BlockSpec(memory_space=pltpu.HBM)] * 6,
        out_specs=vmem,
        scratch_shapes=[
            pltpu.VMEM((1, 2 * half), jnp.int32),
            pltpu.SMEM(band_mask.shape, jnp.int32),
            pltpu.VMEM((1, rows), bf16),
            pltpu.VMEM((4 * part, rows), bf16),
            pltpu.VMEM((floors, 2, 2, half, width), bf16),
            pltpu.VMEM((floors, clusters, half), f32),
            pltpu.VMEM((4 * rows, depth), bf16),
            pltpu.VMEM((4, 2, 2, padded, rows), bf16),
            pltpu.VMEM((4, 8, rows), f32),
            pltpu.VMEM((4 * rows, half), f32),
            pltpu.VMEM((floors, 4 * rows, half), bf16),
            pltpu.VMEM((floors, 8, half), f32),
            pltpu.VMEM((floors, 2, padded, half), bf16),
            pltpu.VMEM((floors, 2, padded, half), bf16),
            pltpu.VMEM((floors, 8, half), f32),
            pltpu.VMEM((floors, 2, padded, half), bf16),
            pltpu.VMEM((floors, 8, half), f32),
            pltpu.VMEM((2 * floors, padded, half), bf16),
            pltpu.VMEM((2 * floors, 8, half), f32),
            pltpu.SemaphoreType.DMA((copies,)),
            pltpu.SemaphoreType.DMA((copies,)),
            pltpu.SemaphoreType.DMA((7, 2 * floors)),
            pltpu.SemaphoreType.DMA((6,)),
        ],
        compiler_params=pltpu.CompilerParams(
            collective_id=0, has_side_effects=True, vmem_limit_bytes=60 * 1024 * 1024
        ),
    )(queries, assign.reshape(1, -1), band_mask, keys, labels.T, prior.reshape(1, -1))


def from_behind(array, axis, by):
    peers = lax.axis_size(axis)
    return lax.ppermute(array, axis, [(i, (i + by) % peers) for i in range(peers)])


def combined_all(part, axis, combine):
    gathered = jax.tree.map(lambda a: lax.all_gather(a, axis), part)

    def take(source):
        return jax.tree.map(lambda a: lax.dynamic_index_in_dim(a, source, 0, False), gathered)

    return lax.fori_loop(
        1, lax.axis_size(axis), lambda source, state: combine(state, take(source)), take(0)
    )


def combine_totals(first, second):
    top_first, sum_first = first
    top_second, sum_second = second
    highest = jnp.maximum(top_first, top_second)
    return (
        highest,
        sum_first * jnp.exp(top_first - highest) + sum_second * jnp.exp(top_second - highest),
    )


def absorb(state, block, query_full, enabled):
    running, total, accum = state
    block_keys, block_labels, block_prior = block
    scale = temper / math.sqrt(query_full.shape[1])
    scores = (
        jnp.einsum("qd,kd->qk", query_full, block_keys, preferred_element_type=jnp.float32) * scale
    )
    scores = scores + block_prior.astype(jnp.float32)[None, :]
    scores = jnp.where(enabled, scores, jnp.float32(-1e30))
    highest = jnp.maximum(running, jnp.max(scores, axis=1))
    carried = jnp.exp(running - highest)
    weight = jnp.exp(scores - highest[:, None])
    total = total * carried + jnp.sum(weight, axis=1)
    accum = accum * carried[:, None] + jnp.dot(
        weight.astype(jnp.bfloat16), block_labels, preferred_element_type=jnp.float32
    )
    return (highest, total, accum)


def body(queries, assign, band_mask, keys, labels, prior):
    clusters = lax.axis_size("cluster")
    cluster_index = lax.axis_index("cluster")
    local_rows = queries.shape[0]
    capacity = 2 * local_rows // clusters
    slots = clusters * capacity
    target = assign[:, 0]
    onehot = (target[:, None] == jnp.arange(clusters, dtype=jnp.int32)[None, :]).astype(jnp.int32)
    before = jnp.cumsum(onehot, axis=0) - onehot
    position = target * capacity + jnp.sum(before * onehot, axis=1)
    outgoing = jnp.zeros((slots, queries.shape[1]), queries.dtype).at[position].set(queries)
    arrived = lax.all_to_all(
        outgoing.reshape(clusters, capacity, queries.shape[1]),
        "cluster",
        split_axis=0,
        concat_axis=0,
        tiled=True,
    )
    query_full = lax.all_gather(
        arrived.reshape(slots, queries.shape[1]), "feat", axis=1, tiled=True
    )
    mask_row = band_mask[cluster_index]
    classes = labels.shape[1]
    state = (
        jnp.full((slots,), -1e30, jnp.float32),
        jnp.zeros((slots,), jnp.float32),
        jnp.zeros((slots, classes), jnp.float32),
    )
    state = absorb(state, (keys, labels, prior), query_full, jnp.bool_(True))

    def visit(current, block, offset):
        enabled = mask_row[REACH + offset] > 0
        return absorb(current, block, query_full, enabled)

    up_keys, up_labels, up_prior = (keys, labels, prior)
    down_keys, down_labels, down_prior = (keys, labels, prior)
    for reach in range(1, REACH + 1):
        up_keys, up_labels, up_prior = from_behind((up_keys, up_labels, up_prior), "cluster", -1)
        state = visit(state, (up_keys, up_labels, up_prior), reach)
        down_keys, down_labels, down_prior = from_behind(
            (down_keys, down_labels, down_prior), "cluster", 1
        )
        state = visit(state, (down_keys, down_labels, down_prior), -reach)
    running, total, accum = state
    highest, grand_total = combined_all((running, total), "feat", combine_totals)
    factor = jnp.exp(running - highest) / grand_total
    shares = lax.psum_scatter(
        (accum * factor[:, None]).astype(jnp.bfloat16), "feat", scatter_dimension=1, tiled=True
    )
    returned = lax.all_to_all(
        shares.reshape(clusters, capacity, shares.shape[1]),
        "cluster",
        split_axis=0,
        concat_axis=0,
        tiled=True,
    )
    return returned.reshape(slots, shares.shape[1])[position]


def solution(mesh):
    in_specs = (
        P("cluster", "feat"),
        P("cluster", None),
        P(),
        P(("cluster", "feat"), None),
        P(("cluster", "feat"), None),
        P(("cluster", "feat")),
    )
    out_specs = P("cluster", "feat")
    planes = mesh.shape["cluster"] == 8 and mesh.shape["feat"] == 4
    return jax.shard_map(plane_body if planes else body, mesh=mesh, in_specs=in_specs, out_specs=out_specs, check_vma=False)
```

```python
import functools
import math

import jax
import jax.numpy as jnp
from jax import lax
from jax.experimental import pallas as pl
from jax.experimental.pallas import tpu as pltpu
from jax.sharding import PartitionSpec as P

REACH = 3
HIDDEN = -1e30
MESH = pl.DeviceIdType.MESH


temper = 2.0


def spread(row, width):
    return jnp.broadcast_to(row, (width, row.shape[1])).T


def plane_kernel(
    scale,
    queries_ref,
    assign_ref,
    mask_ref,
    keys_ref,
    labels_ref,
    prior_ref,
    out_ref,
    assign_buf,
    mask_buf,
    prior_buf,
    labels_buf,
    qbuf,
    vbuf,
    kbuf,
    lbuf,
    pbuf,
    bias,
    weights,
    stats_own,
    numer_out,
    numer_in,
    stats_in,
    home_out,
    home_stats_out,
    home_in,
    home_stats_in,
    send_sem,
    recv_sem,
    home_sem,
    load_sem,
):
    cluster = lax.axis_index("cluster")
    feat = lax.axis_index("feat")
    clusters = mask_ref.shape[0]
    floors = clusters // 2
    half = queries_ref.shape[0] // 2
    rows = keys_ref.shape[0]
    part = labels_ref.shape[0] // 4
    padded = lbuf.shape[3]
    z, y = lax.div(cluster, 2), lax.rem(cluster, 2)
    x, core = lax.div(feat, 2), lax.rem(feat, 2)
    twin = (cluster, feat + 1 - 2 * core)
    across = (cluster, feat + 2 - 4 * x)
    beside = (cluster + 1 - 2 * y, feat)

    def mate(peer):
        return (peer[0], peer[1] + 1 - 2 * core)

    above, below = (cluster + 2, feat), (cluster - 2, feat)
    FIRST, SECOND, EXTRA, ACROSS, SEEN, NUMER, STATS = range(7)

    loads = [
        pltpu.make_async_copy(src, dst, load_sem.at[index])
        for index, (src, dst) in enumerate(
            [
                (queries_ref.at[pl.ds(core * half, half)], qbuf.at[z, x, core]),
                (prior_ref, prior_buf),
                (labels_ref, labels_buf),
                (mask_ref, mask_buf),
                (assign_ref, assign_buf),
                (keys_ref, kbuf.at[pl.ds(0, rows)]),
            ]
        )
    ]
    for load in loads:
        load.start()

    inner = jnp.minimum(z, floors - 1 - z)
    upper = lax.div(z, 2)

    def home_at(step):
        if step == 0:
            return z
        near = step - inner if step == 1 else step + 0 * inner
        return near + upper * (floors - 1 - 2 * near)

    homes = [home_at(step) for step in range(floors)]

    def floor_peer(floor):
        return (2 * floor + y, feat)

    barrier = pltpu.get_barrier_semaphore()
    peers = [twin, across, mate(across), beside]
    for home in homes[1:]:
        peers += [floor_peer(home), mate(floor_peer(home))]
    for peer in peers:
        pl.semaphore_signal(barrier, inc=1, device_id=peer, device_id_type=MESH)
    pl.semaphore_wait(barrier, len(peers))

    started = []

    def send(src, dst, peer, where=None, only=None):
        index = len(started)
        copy = pltpu.make_async_remote_copy(
            src_ref=src,
            dst_ref=dst,
            send_sem=send_sem.at[index],
            recv_sem=recv_sem.at[index] if where is None else home_sem.at[where[0], where[1]],
            device_id=peer,
            device_id_type=MESH,
        )
        started.append((copy, only))
        if only is None:
            copy.start()
        else:
            pl.when(only)(copy.start)
        return copy

    def arrived(ref, kind, index, only=None):
        copy = pltpu.make_async_remote_copy(
            src_ref=ref,
            dst_ref=ref,
            send_sem=send_sem.at[0],
            recv_sem=home_sem.at[kind, index],
            device_id=twin,
            device_id_type=MESH,
        )
        if only is None:
            copy.wait_recv()
        else:
            pl.when(only)(copy.wait_recv)

    mine = pl.ds(pl.multiple_of(core * half, half), half)
    other = pl.ds(pl.multiple_of((1 - core) * half, half), half)
    up, down = z < floors - 1, z > 0

    def block(index):
        return pl.ds(index * rows, rows)

    own, piece = qbuf.at[z, x, core], core
    query_twin = send(queries_ref.at[other], own, twin)
    send(queries_ref.at[mine], own, above, (FIRST + piece, z), up)
    send(queries_ref.at[mine], own, below, (FIRST + piece, z), down)
    send(queries_ref.at[other], own, mate(above), (FIRST + piece, z), up)
    send(queries_ref.at[other], own, mate(below), (FIRST + piece, z), down)
    send(queries_ref.at[mine], own, across, (FIRST + piece, z))
    send(queries_ref.at[other], own, mate(across), (FIRST + piece, z))
    keys_beside = send(keys_ref, kbuf.at[block(2)], beside)
    keys_twin = send(keys_ref, kbuf.at[block(1)], twin)
    loads[1].wait()
    pbuf[0] = jnp.broadcast_to(prior_buf[...].astype(jnp.float32), (8, rows))
    prior_beside = send(pbuf.at[0], pbuf.at[2], beside)
    prior_twin = send(pbuf.at[0], pbuf.at[1], twin)

    def pass_on(home, kind, ref, only):
        send(ref, ref, above, (kind, home), only & (home <= z) & up)
        send(ref, ref, below, (kind, home), only & (home >= z) & down)

    lbuf[0] = jnp.zeros(lbuf.shape[1:], lbuf.dtype)
    loads[2].wait()
    for quarter in range(4):
        lbuf[0, quarter // 2, quarter % 2, :part, :] = labels_buf[
            quarter * part : (quarter + 1) * part, :
        ]
    quarters = [(1 - x, 0), (1 - x, 1), (x, 0), (x, 1)]
    labels_beside, labels_twin, labels_relay = [], [], []
    for side, turn in quarters:
        labels_beside.append(send(lbuf.at[0, side, turn], lbuf.at[2, side, turn], beside))
        labels_twin.append(send(lbuf.at[0, side, turn], lbuf.at[1, side, turn], twin))

    def relay_labels(index):
        side, turn = quarters[index]
        labels_beside[index].wait_recv()
        labels_relay.append(send(lbuf.at[2, side, turn], lbuf.at[3, side, turn], twin))

    def labels_here(index):
        labels_twin[index].wait_recv()
        labels_relay[index].wait_recv()

    loads[3].wait()
    loads[4].wait()
    assigned = assign_buf[...]
    assigned = jnp.where(core == 0, assigned[:, :half], assigned[:, half:])
    assigned = jnp.broadcast_to(assigned, (clusters, half))
    row = lax.broadcasted_iota(jnp.int32, (clusters, half), 0)
    seen = jnp.zeros((clusters, half), jnp.int32)
    for owner in range(clusters):
        column = jnp.zeros((clusters, half), jnp.int32)
        for step in range(2 * REACH + 1):
            column = jnp.where(
                row == (owner + step - REACH) % clusters, mask_buf[owner, step], column
            )
        seen = jnp.where(assigned == owner, column, seen)
    vbuf[z] = jnp.where(seen > 0, jnp.float32(0.0), jnp.float32(HIDDEN))
    for home in homes[1:]:
        send(vbuf.at[z], vbuf.at[z], floor_peer(home), (SEEN, z))

    def relay(step, only):
        home = homes[step]
        first, second, extra = qbuf.at[home, x, 0], qbuf.at[home, x, 1], qbuf.at[home, 1 - x, 1]
        arrived(first, FIRST, home, only)
        pass_on(home, FIRST, first, only)
        send(first, first, across, (ACROSS, home), only)
        arrived(second, SECOND, home, only)
        pass_on(home, SECOND, second, only)
        arrived(extra, EXTRA, home, only)
        pass_on(home, EXTRA, extra, only)

    def score(step):
        home = homes[step]
        if step > 0:
            arrived(qbuf.at[home, 1 - x, 0], ACROSS, home)
            arrived(vbuf.at[home], SEEN, home)
        width = qbuf.shape[4]
        scores = jnp.zeros((4 * rows, half), jnp.float32)
        for quarter in range(4):
            scores = scores + lax.dot_general(
                kbuf[:, quarter * width : (quarter + 1) * width],
                qbuf[home, quarter // 2, quarter % 2],
                (((1,), (1,)), ((), ())),
                preferred_element_type=jnp.float32,
            )
        scores = scores * scale
        near = vbuf[home, pl.ds(cluster, 1), :]
        far = vbuf[home, pl.ds(cluster + 1 - 2 * y, 1), :]
        pieces = []
        for index in range(4):
            cut = slice(index * rows, (index + 1) * rows)
            pieces.append(scores[cut] + bias[cut, :] + (near if index < 2 else far))
        scores = jnp.concatenate(pieces, axis=0)
        top = jnp.max(scores, axis=0, keepdims=True)
        weight = jnp.exp(scores - top)
        total = jnp.sum(weight, axis=0, keepdims=True)
        weights[step] = weight.astype(jnp.bfloat16)
        stats_own[step, 0:1, :] = top
        stats_own[step, 1:2, :] = total
        stats_own[step, 2:8, :] = jnp.zeros((6, half), jnp.float32)

    def class_sum(step, side, turn):
        blocks = jnp.concatenate([lbuf[index, side, turn] for index in range(4)], axis=1)
        return jnp.dot(blocks, weights[step], preferred_element_type=jnp.float32)

    numer_across, stats_across, carried = {}, {}, {}

    def send_across(step, turn):
        numer_out[step, turn] = class_sum(step, 1 - x, turn).astype(jnp.bfloat16)
        if turn == 0:
            stats_across[step] = send(stats_own.at[step], stats_in.at[step], across)
        numer_across[step, turn] = send(
            numer_out.at[step, turn], numer_in.at[step, turn], across
        )

    place = 2 * z + core

    def merge(step, turn):
        numer = class_sum(step, x, turn)
        floor = homes[step]
        if turn == 0:
            stats_across[step].wait_recv()
            top_own, top_in = stats_own[step, 0:1, :], stats_in[step, 0:1, :]
            top = jnp.maximum(top_own, top_in)
            carry_own, carry_in = jnp.exp(top_own - top), jnp.exp(top_in - top)
            total = stats_own[step, 1:2, :] * carry_own + stats_in[step, 1:2, :] * carry_in
            carried[step] = carry_own, carry_in
            home_stats_out[step, 0:1, :] = top
            home_stats_out[step, 1:2, :] = total
            home_stats_out[step, 2:8, :] = jnp.zeros((6, half), jnp.float32)
            if step > 0:
                for peer in (floor_peer(floor), mate(floor_peer(floor))):
                    send(home_stats_out.at[step], home_stats_in.at[place], peer, (STATS, place))
            else:
                home_stats_in[place] = home_stats_out[0]
                send(home_stats_out.at[0], home_stats_in.at[place], twin, (STATS, place))
        carry_own, carry_in = carried[step]
        numer_across[step, turn].wait_recv()
        merged = numer * carry_own + numer_in[step, turn].astype(jnp.float32) * carry_in
        home_out[step, turn] = merged.astype(jnp.bfloat16)
        if step > 0:
            peer = (2 * floor + y, 2 * x + turn)
            send(home_out.at[step, turn], home_in.at[place], peer, (NUMER, place))
        elif turn == 1:
            home_in[place] = home_out[0, core]
            send(home_out.at[0, 1 - core], home_in.at[place], twin, (NUMER, place))

    always, inside = z >= 0, inner > 0
    arrived(qbuf.at[z, 1 - x, 0], FIRST, z)
    arrived(qbuf.at[z, 1 - x, 1], SECOND, z)
    pass_on(z, EXTRA, qbuf.at[z, 1 - x, 1], always)
    relay(1, always)
    relay(2, always)
    keys_beside.wait_recv()
    prior_beside.wait_recv()
    keys_relay = send(kbuf.at[block(2)], kbuf.at[block(3)], twin)
    prior_relay = send(pbuf.at[2], pbuf.at[3], twin)
    for copy in (keys_twin, prior_twin, keys_relay, prior_relay, query_twin):
        copy.wait_recv()
    loads[0].wait()
    loads[5].wait()
    for index in range(4):
        bias[block(index), :] = spread(pbuf[index, 0:1, :], half)
    score(0)
    relay(3, inside)
    score(1)
    relay_labels(0)
    score(2)
    labels_here(0)
    send_across(2, 0)
    relay_labels(1)
    relay(3, inner == 0)
    labels_here(1)
    send_across(2, 1)
    score(3)
    send_across(3, 0)
    send_across(3, 1)
    relay_labels(2)
    send_across(1, 0)
    send_across(1, 1)
    labels_here(2)
    merge(2, 0)
    relay_labels(3)
    labels_here(3)
    merge(2, 1)
    merge(3, 0)
    send_across(0, 0)
    send_across(0, 1)
    merge(3, 1)
    for step in (1, 0):
        merge(step, 0)
        merge(step, 1)

    for side in (0, 1):
        source = core if side == 0 else 1 - core
        places = [2 * home + source for home in homes]
        for step in range(floors):
            if side + step > 0:
                arrived(home_stats_in.at[places[step]], STATS, places[step])
        tops = [home_stats_in[place, 0:1, :] for place in places]
        totals = [home_stats_in[place, 1:2, :] for place in places]
        top = functools.reduce(jnp.maximum, tops)
        carries = [jnp.exp(t - top) for t in tops]
        total = functools.reduce(jnp.add, [t * c for t, c in zip(totals, carries)])
        result = jnp.zeros((padded, half), jnp.float32)
        for step in range(floors):
            if side + step > 0:
                arrived(home_in.at[places[step]], NUMER, places[step])
            result = result + home_in[places[step]].astype(jnp.float32) * (carries[step] / total)
        out_ref[mine if side == 0 else other, :] = result.T.astype(jnp.bfloat16)[:, :part]
    for copy, only in started:
        if only is None:
            copy.wait_send()
        else:
            pl.when(only)(copy.wait_send)


def plane_body(queries, assign, band_mask, keys, labels, prior):
    clusters = lax.axis_size("cluster")
    floors = clusters // 2
    half, width = queries.shape[0] // 2, queries.shape[1]
    rows, depth = keys.shape
    part = labels.shape[1] // 4
    padded = -(-part // 128) * 128
    vmem = pl.BlockSpec(memory_space=pltpu.VMEM)
    bf16, f32 = jnp.bfloat16, jnp.float32
    copies = 112
    return pl.pallas_call(
        functools.partial(plane_kernel, temper / math.sqrt(depth)),
        out_shape=jax.ShapeDtypeStruct((2 * half, part), bf16),
        in_specs=[pl.BlockSpec(memory_space=pltpu.HBM)] * 6,
        out_specs=vmem,
        scratch_shapes=[
            pltpu.VMEM((1, 2 * half), jnp.int32),
            pltpu.SMEM(band_mask.shape, jnp.int32),
            pltpu.VMEM((1, rows), bf16),
            pltpu.VMEM((4 * part, rows), bf16),
            pltpu.VMEM((floors, 2, 2, half, width), bf16),
            pltpu.VMEM((floors, clusters, half), f32),
            pltpu.VMEM((4 * rows, depth), bf16),
            pltpu.VMEM((4, 2, 2, padded, rows), bf16),
            pltpu.VMEM((4, 8, rows), f32),
            pltpu.VMEM((4 * rows, half), f32),
            pltpu.VMEM((floors, 4 * rows, half), bf16),
            pltpu.VMEM((floors, 8, half), f32),
            pltpu.VMEM((floors, 2, padded, half), bf16),
            pltpu.VMEM((floors, 2, padded, half), bf16),
            pltpu.VMEM((floors, 8, half), f32),
            pltpu.VMEM((floors, 2, padded, half), bf16),
            pltpu.VMEM((floors, 8, half), f32),
            pltpu.VMEM((2 * floors, padded, half), bf16),
            pltpu.VMEM((2 * floors, 8, half), f32),
            pltpu.SemaphoreType.DMA((copies,)),
            pltpu.SemaphoreType.DMA((copies,)),
            pltpu.SemaphoreType.DMA((7, 2 * floors)),
            pltpu.SemaphoreType.DMA((6,)),
        ],
        compiler_params=pltpu.CompilerParams(
            collective_id=0, has_side_effects=True, vmem_limit_bytes=60 * 1024 * 1024
        ),
    )(queries, assign.reshape(1, -1), band_mask, keys, labels.T, prior.reshape(1, -1))


def from_behind(array, axis, by):
    peers = lax.axis_size(axis)
    return lax.ppermute(array, axis, [(i, (i + by) % peers) for i in range(peers)])


def combined_all(part, axis, combine):
    gathered = jax.tree.map(lambda a: lax.all_gather(a, axis), part)

    def take(source):
        return jax.tree.map(lambda a: lax.dynamic_index_in_dim(a, source, 0, False), gathered)

    return lax.fori_loop(
        1, lax.axis_size(axis), lambda source, state: combine(state, take(source)), take(0)
    )


def combine_totals(first, second):
    top_first, sum_first = first
    top_second, sum_second = second
    highest = jnp.maximum(top_first, top_second)
    return (
        highest,
        sum_first * jnp.exp(top_first - highest) + sum_second * jnp.exp(top_second - highest),
    )


def absorb(state, block, query_full, enabled):
    running, total, accum = state
    block_keys, block_labels, block_prior = block
    scale = temper / math.sqrt(query_full.shape[1])
    scores = (
        jnp.einsum("qd,kd->qk", query_full, block_keys, preferred_element_type=jnp.float32) * scale
    )
    scores = scores + block_prior.astype(jnp.float32)[None, :]
    scores = jnp.where(enabled, scores, jnp.float32(-1e30))
    highest = jnp.maximum(running, jnp.max(scores, axis=1))
    carried = jnp.exp(running - highest)
    weight = jnp.exp(scores - highest[:, None])
    total = total * carried + jnp.sum(weight, axis=1)
    accum = accum * carried[:, None] + jnp.dot(
        weight.astype(jnp.bfloat16), block_labels, preferred_element_type=jnp.float32
    )
    return (highest, total, accum)


def body(queries, assign, band_mask, keys, labels, prior):
    clusters = lax.axis_size("cluster")
    cluster_index = lax.axis_index("cluster")
    local_rows = queries.shape[0]
    capacity = 2 * local_rows // clusters
    slots = clusters * capacity
    target = assign[:, 0]
    onehot = (target[:, None] == jnp.arange(clusters, dtype=jnp.int32)[None, :]).astype(jnp.int32)
    before = jnp.cumsum(onehot, axis=0) - onehot
    position = target * capacity + jnp.sum(before * onehot, axis=1)
    outgoing = jnp.zeros((slots, queries.shape[1]), queries.dtype).at[position].set(queries)
    arrived = lax.all_to_all(
        outgoing.reshape(clusters, capacity, queries.shape[1]),
        "cluster",
        split_axis=0,
        concat_axis=0,
        tiled=True,
    )
    query_full = lax.all_gather(
        arrived.reshape(slots, queries.shape[1]), "feat", axis=1, tiled=True
    )
    mask_row = band_mask[cluster_index]
    classes = labels.shape[1]
    state = (
        jnp.full((slots,), -1e30, jnp.float32),
        jnp.zeros((slots,), jnp.float32),
        jnp.zeros((slots, classes), jnp.float32),
    )
    state = absorb(state, (keys, labels, prior), query_full, jnp.bool_(True))

    def visit(current, block, offset):
        enabled = mask_row[REACH + offset] > 0
        return absorb(current, block, query_full, enabled)

    up_keys, up_labels, up_prior = (keys, labels, prior)
    down_keys, down_labels, down_prior = (keys, labels, prior)
    for reach in range(1, REACH + 1):
        up_keys, up_labels, up_prior = from_behind((up_keys, up_labels, up_prior), "cluster", -1)
        state = visit(state, (up_keys, up_labels, up_prior), reach)
        down_keys, down_labels, down_prior = from_behind(
            (down_keys, down_labels, down_prior), "cluster", 1
        )
        state = visit(state, (down_keys, down_labels, down_prior), -reach)
    running, total, accum = state
    highest, grand_total = combined_all((running, total), "feat", combine_totals)
    factor = jnp.exp(running - highest) / grand_total
    shares = lax.psum_scatter(
        (accum * factor[:, None]).astype(jnp.bfloat16), "feat", scatter_dimension=1, tiled=True
    )
    returned = lax.all_to_all(
        shares.reshape(clusters, capacity, shares.shape[1]),
        "cluster",
        split_axis=0,
        concat_axis=0,
        tiled=True,
    )
    return returned.reshape(slots, shares.shape[1])[position]


def solution(mesh):
    in_specs = (
        P("cluster", "feat"),
        P("cluster", None),
        P(),
        P(("cluster", "feat"), None),
        P(("cluster", "feat"), None),
        P(("cluster", "feat")),
    )
    out_specs = P("cluster", "feat")
    planes = mesh.shape["cluster"] == 8 and mesh.shape["feat"] == 4
    return jax.shard_map(plane_body if planes else body, mesh=mesh, in_specs=in_specs, out_specs=out_specs, check_vma=False)
```

```python
import functools
import math

import jax
import jax.numpy as jnp
from jax import lax
from jax.experimental import pallas as pl
from jax.experimental.pallas import tpu as pltpu
from jax.sharding import PartitionSpec as P

REACH = 3
HIDDEN = -1e30
MESH = pl.DeviceIdType.MESH


temper = 2.0


def spread(row, width):
    return jnp.broadcast_to(row, (width, row.shape[1])).T


def plane_kernel(
    scale,
    queries_ref,
    assign_ref,
    mask_ref,
    keys_ref,
    labels_ref,
    prior_ref,
    out_ref,
    assign_buf,
    mask_buf,
    prior_buf,
    labels_buf,
    qbuf,
    vbuf,
    kbuf,
    lbuf,
    pbuf,
    bias,
    weights,
    stats_own,
    numer_out,
    numer_in,
    stats_in,
    home_out,
    home_stats_out,
    home_in,
    home_stats_in,
    send_sem,
    recv_sem,
    home_sem,
    load_sem,
):
    cluster = lax.axis_index("cluster")
    feat = lax.axis_index("feat")
    clusters = mask_ref.shape[0]
    floors = clusters // 2
    half = queries_ref.shape[0] // 2
    rows = keys_ref.shape[0]
    part = labels_ref.shape[0] // 4
    padded = lbuf.shape[3]
    z, y = lax.div(cluster, 2), lax.rem(cluster, 2)
    x, core = lax.div(feat, 2), lax.rem(feat, 2)
    twin = (cluster, feat + 1 - 2 * core)
    across = (cluster, feat + 2 - 4 * x)
    beside = (cluster + 1 - 2 * y, feat)

    def mate(peer):
        return (peer[0], peer[1] + 1 - 2 * core)

    above, below = (cluster + 2, feat), (cluster - 2, feat)
    FIRST, SECOND, ACROSS, ACROSS_SECOND, SEEN, NUMER, STATS = range(7)

    loads = [
        pltpu.make_async_copy(src, dst, load_sem.at[index])
        for index, (src, dst) in enumerate(
            [
                (queries_ref.at[pl.ds(core * half, half)], qbuf.at[z, x, core]),
                (prior_ref, prior_buf),
                (labels_ref, labels_buf),
                (mask_ref, mask_buf),
                (assign_ref, assign_buf),
                (keys_ref, kbuf.at[pl.ds(0, rows)]),
            ]
        )
    ]
    for load in loads:
        load.start()

    inner = jnp.minimum(z, floors - 1 - z)
    upper = lax.div(z, 2)

    def home_at(step):
        if step == 0:
            return z
        near = step - inner if step == 1 else step + 0 * inner
        return near + upper * (floors - 1 - 2 * near)

    homes = [home_at(step) for step in range(floors)]

    def floor_peer(floor):
        return (2 * floor + y, feat)

    barrier = pltpu.get_barrier_semaphore()
    peers = [twin, across, mate(across), beside]
    for home in homes[1:]:
        peers += [floor_peer(home), mate(floor_peer(home))]
    for peer in peers:
        pl.semaphore_signal(barrier, inc=1, device_id=peer, device_id_type=MESH)
    pl.semaphore_wait(barrier, len(peers))

    started = []

    def send(src, dst, peer, where=None, only=None):
        index = len(started)
        copy = pltpu.make_async_remote_copy(
            src_ref=src,
            dst_ref=dst,
            send_sem=send_sem.at[index],
            recv_sem=recv_sem.at[index] if where is None else home_sem.at[where[0], where[1]],
            device_id=peer,
            device_id_type=MESH,
        )
        started.append((copy, only))
        if only is None:
            copy.start()
        else:
            pl.when(only)(copy.start)
        return copy

    def arrived(ref, kind, index, only=None):
        copy = pltpu.make_async_remote_copy(
            src_ref=ref,
            dst_ref=ref,
            send_sem=send_sem.at[0],
            recv_sem=home_sem.at[kind, index],
            device_id=twin,
            device_id_type=MESH,
        )
        if only is None:
            copy.wait_recv()
        else:
            pl.when(only)(copy.wait_recv)

    mine = pl.ds(pl.multiple_of(core * half, half), half)
    other = pl.ds(pl.multiple_of((1 - core) * half, half), half)
    up, down = z < floors - 1, z > 0

    def block(index):
        return pl.ds(index * rows, rows)

    own, piece = qbuf.at[z, x, core], core
    query_twin = send(queries_ref.at[other], own, twin)
    send(queries_ref.at[mine], own, above, (FIRST + piece, z), up)
    send(queries_ref.at[mine], own, below, (FIRST + piece, z), down)
    send(queries_ref.at[other], own, mate(above), (FIRST + piece, z), up)
    send(queries_ref.at[other], own, mate(below), (FIRST + piece, z), down)
    send(queries_ref.at[mine], own, across, (FIRST + piece, z))
    send(queries_ref.at[other], own, mate(across), (FIRST + piece, z))
    keys_beside = send(keys_ref, kbuf.at[block(2)], beside)
    keys_twin = send(keys_ref, kbuf.at[block(1)], twin)
    loads[1].wait()
    pbuf[0] = jnp.broadcast_to(prior_buf[...].astype(jnp.float32), (8, rows))
    prior_beside = send(pbuf.at[0], pbuf.at[2], beside)
    prior_twin = send(pbuf.at[0], pbuf.at[1], twin)

    def pass_on(home, kind, ref, only):
        send(ref, ref, above, (kind, home), only & (home <= z) & up)
        send(ref, ref, below, (kind, home), only & (home >= z) & down)

    lbuf[0] = jnp.zeros(lbuf.shape[1:], lbuf.dtype)
    loads[2].wait()
    for quarter in range(4):
        lbuf[0, quarter // 2, quarter % 2, :part, :] = labels_buf[
            quarter * part : (quarter + 1) * part, :
        ]
    quarters = [(1 - x, 0), (1 - x, 1), (x, 0), (x, 1)]
    labels_beside, labels_twin, labels_relay = [], [], []
    for side, turn in quarters:
        labels_beside.append(send(lbuf.at[0, side, turn], lbuf.at[2, side, turn], beside))
        labels_twin.append(send(lbuf.at[0, side, turn], lbuf.at[1, side, turn], twin))

    def relay_labels(index):
        side, turn = quarters[index]
        labels_beside[index].wait_recv()
        labels_relay.append(send(lbuf.at[2, side, turn], lbuf.at[3, side, turn], twin))

    def labels_here(index):
        labels_twin[index].wait_recv()
        labels_relay[index].wait_recv()

    loads[3].wait()
    loads[4].wait()
    assigned = assign_buf[...]
    assigned = jnp.where(core == 0, assigned[:, :half], assigned[:, half:])
    assigned = jnp.broadcast_to(assigned, (clusters, half))
    row = lax.broadcasted_iota(jnp.int32, (clusters, half), 0)
    seen = jnp.zeros((clusters, half), jnp.int32)
    for owner in range(clusters):
        column = jnp.zeros((clusters, half), jnp.int32)
        for step in range(2 * REACH + 1):
            column = jnp.where(
                row == (owner + step - REACH) % clusters, mask_buf[owner, step], column
            )
        seen = jnp.where(assigned == owner, column, seen)
    vbuf[z] = jnp.where(seen > 0, jnp.float32(0.0), jnp.float32(HIDDEN))
    for home in homes[1:]:
        send(vbuf.at[z], vbuf.at[z], floor_peer(home), (SEEN, z))

    def relay(step, only):
        home = homes[step]
        for turn, (kind, copied) in enumerate(((FIRST, ACROSS), (SECOND, ACROSS_SECOND))):
            part_here = qbuf.at[home, x, turn]
            arrived(part_here, kind, home, only)
            pass_on(home, kind, part_here, only)
            send(part_here, part_here, across, (copied, home), only)

    def score(step):
        home = homes[step]
        if step > 0:
            arrived(qbuf.at[home, 1 - x, 0], ACROSS, home)
            arrived(qbuf.at[home, 1 - x, 1], ACROSS_SECOND, home)
            arrived(vbuf.at[home], SEEN, home)
        width = qbuf.shape[4]
        scores = jnp.zeros((4 * rows, half), jnp.float32)
        for quarter in range(4):
            scores = scores + lax.dot_general(
                kbuf[:, quarter * width : (quarter + 1) * width],
                qbuf[home, quarter // 2, quarter % 2],
                (((1,), (1,)), ((), ())),
                preferred_element_type=jnp.float32,
            )
        scores = scores * scale
        near = vbuf[home, pl.ds(cluster, 1), :]
        far = vbuf[home, pl.ds(cluster + 1 - 2 * y, 1), :]
        pieces = []
        for index in range(4):
            cut = slice(index * rows, (index + 1) * rows)
            pieces.append(scores[cut] + bias[cut, :] + (near if index < 2 else far))
        scores = jnp.concatenate(pieces, axis=0)
        top = jnp.max(scores, axis=0, keepdims=True)
        weight = jnp.exp(scores - top)
        total = jnp.sum(weight, axis=0, keepdims=True)
        weights[step] = weight.astype(jnp.bfloat16)
        stats_own[step, 0:1, :] = top
        stats_own[step, 1:2, :] = total
        stats_own[step, 2:8, :] = jnp.zeros((6, half), jnp.float32)

    def class_sum(step, side, turn):
        blocks = jnp.concatenate([lbuf[index, side, turn] for index in range(4)], axis=1)
        return jnp.dot(blocks, weights[step], preferred_element_type=jnp.float32)

    numer_across, stats_across, carried = {}, {}, {}

    def send_across(step, turn):
        numer_out[step, turn] = class_sum(step, 1 - x, turn).astype(jnp.bfloat16)
        if turn == 0:
            stats_across[step] = send(stats_own.at[step], stats_in.at[step], across)
        numer_across[step, turn] = send(
            numer_out.at[step, turn], numer_in.at[step, turn], across
        )

    place = 2 * z + core

    def merge(step, turn):
        numer = class_sum(step, x, turn)
        floor = homes[step]
        if turn == 0:
            stats_across[step].wait_recv()
            top_own, top_in = stats_own[step, 0:1, :], stats_in[step, 0:1, :]
            top = jnp.maximum(top_own, top_in)
            carry_own, carry_in = jnp.exp(top_own - top), jnp.exp(top_in - top)
            total = stats_own[step, 1:2, :] * carry_own + stats_in[step, 1:2, :] * carry_in
            carried[step] = carry_own, carry_in
            home_stats_out[step, 0:1, :] = top
            home_stats_out[step, 1:2, :] = total
            home_stats_out[step, 2:8, :] = jnp.zeros((6, half), jnp.float32)
            if step > 0:
                for peer in (floor_peer(floor), mate(floor_peer(floor))):
                    send(home_stats_out.at[step], home_stats_in.at[place], peer, (STATS, place))
            else:
                home_stats_in[place] = home_stats_out[0]
                send(home_stats_out.at[0], home_stats_in.at[place], twin, (STATS, place))
        carry_own, carry_in = carried[step]
        numer_across[step, turn].wait_recv()
        merged = numer * carry_own + numer_in[step, turn].astype(jnp.float32) * carry_in
        home_out[step, turn] = merged.astype(jnp.bfloat16)
        if step > 0:
            peer = (2 * floor + y, 2 * x + turn)
            send(home_out.at[step, turn], home_in.at[place], peer, (NUMER, place))
        elif turn == 1:
            home_in[place] = home_out[0, core]
            send(home_out.at[0, 1 - core], home_in.at[place], twin, (NUMER, place))

    always, inside, at_end = z >= 0, inner > 0, inner == 0
    relay(1, always)
    relay(2, inside)
    keys_beside.wait_recv()
    prior_beside.wait_recv()
    keys_relay = send(kbuf.at[block(2)], kbuf.at[block(3)], twin)
    prior_relay = send(pbuf.at[2], pbuf.at[3], twin)
    relay(3, inside)
    relay(2, at_end)
    arrived(qbuf.at[z, 1 - x, 0], FIRST, z)
    arrived(qbuf.at[z, 1 - x, 1], SECOND, z)
    for copy in (keys_twin, prior_twin, keys_relay, prior_relay, query_twin):
        copy.wait_recv()
    loads[0].wait()
    loads[5].wait()
    for index in range(4):
        bias[block(index), :] = spread(pbuf[index, 0:1, :], half)
    score(0)
    score(1)
    relay_labels(0)
    score(2)
    labels_here(0)
    send_across(2, 0)
    relay_labels(1)
    relay(3, at_end)
    labels_here(1)
    send_across(2, 1)
    score(3)
    send_across(3, 0)
    send_across(3, 1)
    relay_labels(2)
    send_across(1, 0)
    send_across(1, 1)
    labels_here(2)
    merge(2, 0)
    relay_labels(3)
    labels_here(3)
    merge(2, 1)
    merge(3, 0)
    send_across(0, 0)
    send_across(0, 1)
    merge(3, 1)
    for step in (1, 0):
        merge(step, 0)
        merge(step, 1)

    for side in (0, 1):
        source = core if side == 0 else 1 - core
        places = [2 * home + source for home in homes]
        for step in range(floors):
            if side + step > 0:
                arrived(home_stats_in.at[places[step]], STATS, places[step])
        tops = [home_stats_in[place, 0:1, :] for place in places]
        totals = [home_stats_in[place, 1:2, :] for place in places]
        top = functools.reduce(jnp.maximum, tops)
        carries = [jnp.exp(t - top) for t in tops]
        total = functools.reduce(jnp.add, [t * c for t, c in zip(totals, carries)])
        result = jnp.zeros((padded, half), jnp.float32)
        for step in range(floors):
            if side + step > 0:
                arrived(home_in.at[places[step]], NUMER, places[step])
            result = result + home_in[places[step]].astype(jnp.float32) * (carries[step] / total)
        out_ref[mine if side == 0 else other, :] = result.T.astype(jnp.bfloat16)[:, :part]
    for copy, only in started:
        if only is None:
            copy.wait_send()
        else:
            pl.when(only)(copy.wait_send)


def plane_body(queries, assign, band_mask, keys, labels, prior):
    clusters = lax.axis_size("cluster")
    floors = clusters // 2
    half, width = queries.shape[0] // 2, queries.shape[1]
    rows, depth = keys.shape
    part = labels.shape[1] // 4
    padded = -(-part // 128) * 128
    vmem = pl.BlockSpec(memory_space=pltpu.VMEM)
    bf16, f32 = jnp.bfloat16, jnp.float32
    copies = 112
    return pl.pallas_call(
        functools.partial(plane_kernel, temper / math.sqrt(depth)),
        out_shape=jax.ShapeDtypeStruct((2 * half, part), bf16),
        in_specs=[pl.BlockSpec(memory_space=pltpu.HBM)] * 6,
        out_specs=vmem,
        scratch_shapes=[
            pltpu.VMEM((1, 2 * half), jnp.int32),
            pltpu.SMEM(band_mask.shape, jnp.int32),
            pltpu.VMEM((1, rows), bf16),
            pltpu.VMEM((4 * part, rows), bf16),
            pltpu.VMEM((floors, 2, 2, half, width), bf16),
            pltpu.VMEM((floors, clusters, half), f32),
            pltpu.VMEM((4 * rows, depth), bf16),
            pltpu.VMEM((4, 2, 2, padded, rows), bf16),
            pltpu.VMEM((4, 8, rows), f32),
            pltpu.VMEM((4 * rows, half), f32),
            pltpu.VMEM((floors, 4 * rows, half), bf16),
            pltpu.VMEM((floors, 8, half), f32),
            pltpu.VMEM((floors, 2, padded, half), bf16),
            pltpu.VMEM((floors, 2, padded, half), bf16),
            pltpu.VMEM((floors, 8, half), f32),
            pltpu.VMEM((floors, 2, padded, half), bf16),
            pltpu.VMEM((floors, 8, half), f32),
            pltpu.VMEM((2 * floors, padded, half), bf16),
            pltpu.VMEM((2 * floors, 8, half), f32),
            pltpu.SemaphoreType.DMA((copies,)),
            pltpu.SemaphoreType.DMA((copies,)),
            pltpu.SemaphoreType.DMA((7, 2 * floors)),
            pltpu.SemaphoreType.DMA((6,)),
        ],
        compiler_params=pltpu.CompilerParams(
            collective_id=0, has_side_effects=True, vmem_limit_bytes=60 * 1024 * 1024
        ),
    )(queries, assign.reshape(1, -1), band_mask, keys, labels.T, prior.reshape(1, -1))


def from_behind(array, axis, by):
    peers = lax.axis_size(axis)
    return lax.ppermute(array, axis, [(i, (i + by) % peers) for i in range(peers)])


def combined_all(part, axis, combine):
    gathered = jax.tree.map(lambda a: lax.all_gather(a, axis), part)

    def take(source):
        return jax.tree.map(lambda a: lax.dynamic_index_in_dim(a, source, 0, False), gathered)

    return lax.fori_loop(
        1, lax.axis_size(axis), lambda source, state: combine(state, take(source)), take(0)
    )


def combine_totals(first, second):
    top_first, sum_first = first
    top_second, sum_second = second
    highest = jnp.maximum(top_first, top_second)
    return (
        highest,
        sum_first * jnp.exp(top_first - highest) + sum_second * jnp.exp(top_second - highest),
    )


def absorb(state, block, query_full, enabled):
    running, total, accum = state
    block_keys, block_labels, block_prior = block
    scale = temper / math.sqrt(query_full.shape[1])
    scores = (
        jnp.einsum("qd,kd->qk", query_full, block_keys, preferred_element_type=jnp.float32) * scale
    )
    scores = scores + block_prior.astype(jnp.float32)[None, :]
    scores = jnp.where(enabled, scores, jnp.float32(-1e30))
    highest = jnp.maximum(running, jnp.max(scores, axis=1))
    carried = jnp.exp(running - highest)
    weight = jnp.exp(scores - highest[:, None])
    total = total * carried + jnp.sum(weight, axis=1)
    accum = accum * carried[:, None] + jnp.dot(
        weight.astype(jnp.bfloat16), block_labels, preferred_element_type=jnp.float32
    )
    return (highest, total, accum)


def body(queries, assign, band_mask, keys, labels, prior):
    clusters = lax.axis_size("cluster")
    cluster_index = lax.axis_index("cluster")
    local_rows = queries.shape[0]
    capacity = 2 * local_rows // clusters
    slots = clusters * capacity
    target = assign[:, 0]
    onehot = (target[:, None] == jnp.arange(clusters, dtype=jnp.int32)[None, :]).astype(jnp.int32)
    before = jnp.cumsum(onehot, axis=0) - onehot
    position = target * capacity + jnp.sum(before * onehot, axis=1)
    outgoing = jnp.zeros((slots, queries.shape[1]), queries.dtype).at[position].set(queries)
    arrived = lax.all_to_all(
        outgoing.reshape(clusters, capacity, queries.shape[1]),
        "cluster",
        split_axis=0,
        concat_axis=0,
        tiled=True,
    )
    query_full = lax.all_gather(
        arrived.reshape(slots, queries.shape[1]), "feat", axis=1, tiled=True
    )
    mask_row = band_mask[cluster_index]
    classes = labels.shape[1]
    state = (
        jnp.full((slots,), -1e30, jnp.float32),
        jnp.zeros((slots,), jnp.float32),
        jnp.zeros((slots, classes), jnp.float32),
    )
    state = absorb(state, (keys, labels, prior), query_full, jnp.bool_(True))

    def visit(current, block, offset):
        enabled = mask_row[REACH + offset] > 0
        return absorb(current, block, query_full, enabled)

    up_keys, up_labels, up_prior = (keys, labels, prior)
    down_keys, down_labels, down_prior = (keys, labels, prior)
    for reach in range(1, REACH + 1):
        up_keys, up_labels, up_prior = from_behind((up_keys, up_labels, up_prior), "cluster", -1)
        state = visit(state, (up_keys, up_labels, up_prior), reach)
        down_keys, down_labels, down_prior = from_behind(
            (down_keys, down_labels, down_prior), "cluster", 1
        )
        state = visit(state, (down_keys, down_labels, down_prior), -reach)
    running, total, accum = state
    highest, grand_total = combined_all((running, total), "feat", combine_totals)
    factor = jnp.exp(running - highest) / grand_total
    shares = lax.psum_scatter(
        (accum * factor[:, None]).astype(jnp.bfloat16), "feat", scatter_dimension=1, tiled=True
    )
    returned = lax.all_to_all(
        shares.reshape(clusters, capacity, shares.shape[1]),
        "cluster",
        split_axis=0,
        concat_axis=0,
        tiled=True,
    )
    return returned.reshape(slots, shares.shape[1])[position]


def solution(mesh):
    in_specs = (
        P("cluster", "feat"),
        P("cluster", None),
        P(),
        P(("cluster", "feat"), None),
        P(("cluster", "feat"), None),
        P(("cluster", "feat")),
    )
    out_specs = P("cluster", "feat")
    planes = mesh.shape["cluster"] == 8 and mesh.shape["feat"] == 4
    return jax.shard_map(plane_body if planes else body, mesh=mesh, in_specs=in_specs, out_specs=out_specs, check_vma=False)
```

```python
import functools
import math

import jax
import jax.numpy as jnp
from jax import lax
from jax.experimental import pallas as pl
from jax.experimental.pallas import tpu as pltpu
from jax.sharding import PartitionSpec as P

REACH = 3
HIDDEN = -1e30
MESH = pl.DeviceIdType.MESH


temper = 2.0


def spread(row, width):
    return jnp.broadcast_to(row, (width, row.shape[1])).T


def plane_kernel(
    scale,
    queries_ref,
    assign_ref,
    mask_ref,
    keys_ref,
    labels_ref,
    prior_ref,
    out_ref,
    assign_buf,
    mask_buf,
    prior_buf,
    labels_buf,
    qbuf,
    vbuf,
    kbuf,
    lbuf,
    pbuf,
    bias,
    weights,
    stats_own,
    numer_out,
    numer_in,
    stats_in,
    home_out,
    home_stats_out,
    home_in,
    home_stats_in,
    send_sem,
    recv_sem,
    home_sem,
    load_sem,
):
    cluster = lax.axis_index("cluster")
    feat = lax.axis_index("feat")
    clusters = mask_ref.shape[0]
    floors = clusters // 2
    half = queries_ref.shape[0] // 2
    rows = keys_ref.shape[0]
    part = labels_ref.shape[0] // 4
    padded = lbuf.shape[3]
    z, y = lax.div(cluster, 2), lax.rem(cluster, 2)
    x, core = lax.div(feat, 2), lax.rem(feat, 2)
    twin = (cluster, feat + 1 - 2 * core)
    across = (cluster, feat + 2 - 4 * x)
    beside = (cluster + 1 - 2 * y, feat)

    def mate(peer):
        return (peer[0], peer[1] + 1 - 2 * core)

    above, below = (cluster + 2, feat), (cluster - 2, feat)
    FIRST, SECOND, ACROSS, ACROSS_SECOND, SEEN, NUMER, STATS = range(7)

    loads = [
        pltpu.make_async_copy(src, dst, load_sem.at[index])
        for index, (src, dst) in enumerate(
            [
                (queries_ref.at[pl.ds(core * half, half)], qbuf.at[z, x, core]),
                (prior_ref, prior_buf),
                (labels_ref, labels_buf),
                (mask_ref, mask_buf),
                (assign_ref, assign_buf),
                (keys_ref, kbuf.at[pl.ds(0, rows)]),
            ]
        )
    ]
    for load in loads:
        load.start()

    inner = jnp.minimum(z, floors - 1 - z)
    upper = lax.div(z, 2)

    def home_at(step):
        if step == 0:
            return z
        near = step - inner if step == 1 else step + 0 * inner
        return near + upper * (floors - 1 - 2 * near)

    homes = [home_at(step) for step in range(floors)]

    def floor_peer(floor):
        return (2 * floor + y, feat)

    barrier = pltpu.get_barrier_semaphore()
    peers = [twin, across, mate(across), beside]
    for home in homes[1:]:
        peers += [floor_peer(home), mate(floor_peer(home))]
    for peer in peers:
        pl.semaphore_signal(barrier, inc=1, device_id=peer, device_id_type=MESH)
    pl.semaphore_wait(barrier, len(peers))

    started = []

    def send(src, dst, peer, where=None, only=None):
        index = len(started)
        copy = pltpu.make_async_remote_copy(
            src_ref=src,
            dst_ref=dst,
            send_sem=send_sem.at[index],
            recv_sem=recv_sem.at[index] if where is None else home_sem.at[where[0], where[1]],
            device_id=peer,
            device_id_type=MESH,
        )
        started.append((copy, only))
        if only is None:
            copy.start()
        else:
            pl.when(only)(copy.start)
        return copy

    def arrived(ref, kind, index, only=None):
        copy = pltpu.make_async_remote_copy(
            src_ref=ref,
            dst_ref=ref,
            send_sem=send_sem.at[0],
            recv_sem=home_sem.at[kind, index],
            device_id=twin,
            device_id_type=MESH,
        )
        if only is None:
            copy.wait_recv()
        else:
            pl.when(only)(copy.wait_recv)

    mine = pl.ds(pl.multiple_of(core * half, half), half)
    other = pl.ds(pl.multiple_of((1 - core) * half, half), half)
    up, down = z < floors - 1, z > 0

    def block(index):
        return pl.ds(index * rows, rows)

    own, piece = qbuf.at[z, x, core], core
    query_twin = send(queries_ref.at[other], own, twin)
    send(queries_ref.at[mine], own, above, (FIRST + piece, z), up)
    send(queries_ref.at[mine], own, below, (FIRST + piece, z), down)
    send(queries_ref.at[other], own, mate(above), (FIRST + piece, z), up)
    send(queries_ref.at[other], own, mate(below), (FIRST + piece, z), down)
    send(queries_ref.at[mine], own, across, (FIRST + piece, z))
    send(queries_ref.at[other], own, mate(across), (FIRST + piece, z))
    keys_beside = send(keys_ref, kbuf.at[block(2)], beside)
    keys_twin = send(keys_ref, kbuf.at[block(1)], twin)
    loads[1].wait()
    pbuf[0] = jnp.broadcast_to(prior_buf[...].astype(jnp.float32), (8, rows))
    prior_beside = send(pbuf.at[0], pbuf.at[2], beside)
    prior_twin = send(pbuf.at[0], pbuf.at[1], twin)

    def pass_on(home, kind, ref, only):
        send(ref, ref, above, (kind, home), only & (home <= z) & up)
        send(ref, ref, below, (kind, home), only & (home >= z) & down)

    lbuf[0] = jnp.zeros(lbuf.shape[1:], lbuf.dtype)
    loads[2].wait()
    for quarter in range(4):
        lbuf[0, quarter // 2, quarter % 2, :part, :] = labels_buf[
            quarter * part : (quarter + 1) * part, :
        ]
    quarters = [(1 - x, 0), (1 - x, 1), (x, 0), (x, 1)]
    labels_beside, labels_twin, labels_relay = [], [], []
    for side, turn in quarters:
        labels_beside.append(send(lbuf.at[0, side, turn], lbuf.at[2, side, turn], beside))
        labels_twin.append(send(lbuf.at[0, side, turn], lbuf.at[1, side, turn], twin))

    def relay_labels(index):
        side, turn = quarters[index]
        labels_beside[index].wait_recv()
        labels_relay.append(send(lbuf.at[2, side, turn], lbuf.at[3, side, turn], twin))

    def labels_here(index):
        labels_twin[index].wait_recv()
        labels_relay[index].wait_recv()

    loads[3].wait()
    loads[4].wait()
    assigned = assign_buf[...]
    assigned = jnp.where(core == 0, assigned[:, :half], assigned[:, half:])
    assigned = jnp.broadcast_to(assigned, (clusters, half))
    row = lax.broadcasted_iota(jnp.int32, (clusters, half), 0)
    seen = jnp.zeros((clusters, half), jnp.int32)
    for owner in range(clusters):
        column = jnp.zeros((clusters, half), jnp.int32)
        for step in range(2 * REACH + 1):
            column = jnp.where(
                row == (owner + step - REACH) % clusters, mask_buf[owner, step], column
            )
        seen = jnp.where(assigned == owner, column, seen)
    vbuf[z] = jnp.where(seen > 0, jnp.float32(0.0), jnp.float32(HIDDEN))
    for home in homes[1:]:
        send(vbuf.at[z], vbuf.at[z], floor_peer(home), (SEEN, z))

    def relay(step, only):
        home = homes[step]
        for turn, (kind, copied) in enumerate(((FIRST, ACROSS), (SECOND, ACROSS_SECOND))):
            part_here = qbuf.at[home, x, turn]
            arrived(part_here, kind, home, only)
            pass_on(home, kind, part_here, only)
            send(part_here, part_here, across, (copied, home), only)

    def score(step):
        home = homes[step]
        if step > 0:
            arrived(qbuf.at[home, 1 - x, 0], ACROSS, home)
            arrived(qbuf.at[home, 1 - x, 1], ACROSS_SECOND, home)
            arrived(vbuf.at[home], SEEN, home)
        features = jnp.concatenate(
            [qbuf[home, quarter // 2, quarter % 2] for quarter in range(4)], axis=1
        )
        scores = scale * lax.dot_general(
            kbuf[...], features, (((1,), (1,)), ((), ())), preferred_element_type=jnp.float32
        )
        near = vbuf[home, pl.ds(cluster, 1), :]
        far = vbuf[home, pl.ds(cluster + 1 - 2 * y, 1), :]
        pieces = []
        for index in range(4):
            cut = slice(index * rows, (index + 1) * rows)
            pieces.append(scores[cut] + bias[cut, :] + (near if index < 2 else far))
        scores = jnp.concatenate(pieces, axis=0)
        top = jnp.max(scores, axis=0, keepdims=True)
        weight = jnp.exp(scores - top)
        total = jnp.sum(weight, axis=0, keepdims=True)
        weights[step] = weight.astype(jnp.bfloat16)
        stats_own[step, 0:1, :] = top
        stats_own[step, 1:2, :] = total
        stats_own[step, 2:8, :] = jnp.zeros((6, half), jnp.float32)

    def class_sum(step, side, turn):
        blocks = jnp.concatenate([lbuf[index, side, turn] for index in range(4)], axis=1)
        return jnp.dot(blocks, weights[step], preferred_element_type=jnp.float32)

    numer_across, stats_across, carried = {}, {}, {}

    def send_across(step, turn):
        numer_out[step, turn] = class_sum(step, 1 - x, turn).astype(jnp.bfloat16)
        if turn == 0:
            stats_across[step] = send(stats_own.at[step], stats_in.at[step], across)
        numer_across[step, turn] = send(
            numer_out.at[step, turn], numer_in.at[step, turn], across
        )

    place = 2 * z + core

    def merge(step, turn):
        numer = class_sum(step, x, turn)
        floor = homes[step]
        if turn == 0:
            stats_across[step].wait_recv()
            top_own, top_in = stats_own[step, 0:1, :], stats_in[step, 0:1, :]
            top = jnp.maximum(top_own, top_in)
            carry_own, carry_in = jnp.exp(top_own - top), jnp.exp(top_in - top)
            total = stats_own[step, 1:2, :] * carry_own + stats_in[step, 1:2, :] * carry_in
            carried[step] = carry_own, carry_in
            home_stats_out[step, 0:1, :] = top
            home_stats_out[step, 1:2, :] = total
            home_stats_out[step, 2:8, :] = jnp.zeros((6, half), jnp.float32)
            if step > 0:
                for peer in (floor_peer(floor), mate(floor_peer(floor))):
                    send(home_stats_out.at[step], home_stats_in.at[place], peer, (STATS, place))
            else:
                home_stats_in[place] = home_stats_out[0]
                send(home_stats_out.at[0], home_stats_in.at[place], twin, (STATS, place))
        carry_own, carry_in = carried[step]
        numer_across[step, turn].wait_recv()
        merged = numer * carry_own + numer_in[step, turn].astype(jnp.float32) * carry_in
        home_out[step, turn] = merged.astype(jnp.bfloat16)
        if step > 0:
            peer = (2 * floor + y, 2 * x + turn)
            send(home_out.at[step, turn], home_in.at[place], peer, (NUMER, place))
        elif turn == 1:
            home_in[place] = home_out[0, core]
            send(home_out.at[0, 1 - core], home_in.at[place], twin, (NUMER, place))

    always, inside, at_end = z >= 0, inner > 0, inner == 0
    relay(1, always)
    relay(2, inside)
    keys_beside.wait_recv()
    prior_beside.wait_recv()
    keys_relay = send(kbuf.at[block(2)], kbuf.at[block(3)], twin)
    prior_relay = send(pbuf.at[2], pbuf.at[3], twin)
    relay(3, inside)
    relay(2, at_end)
    arrived(qbuf.at[z, 1 - x, 0], FIRST, z)
    arrived(qbuf.at[z, 1 - x, 1], SECOND, z)
    for copy in (keys_twin, prior_twin, keys_relay, prior_relay, query_twin):
        copy.wait_recv()
    loads[0].wait()
    loads[5].wait()
    for index in range(4):
        bias[block(index), :] = spread(pbuf[index, 0:1, :], half)
    score(1)
    relay_labels(0)
    score(2)
    labels_here(0)
    send_across(2, 0)
    relay_labels(1)
    relay(3, at_end)
    labels_here(1)
    send_across(2, 1)
    score(3)
    send_across(3, 0)
    send_across(3, 1)
    score(0)
    relay_labels(2)
    send_across(1, 0)
    send_across(1, 1)
    labels_here(2)
    merge(2, 0)
    relay_labels(3)
    labels_here(3)
    merge(2, 1)
    merge(3, 0)
    send_across(0, 0)
    send_across(0, 1)
    merge(3, 1)
    for step in (1, 0):
        merge(step, 0)
        merge(step, 1)

    for side in (0, 1):
        source = core if side == 0 else 1 - core
        places = [2 * home + source for home in homes]
        for step in range(floors):
            if side + step > 0:
                arrived(home_stats_in.at[places[step]], STATS, places[step])
        tops = [home_stats_in[place, 0:1, :] for place in places]
        totals = [home_stats_in[place, 1:2, :] for place in places]
        top = functools.reduce(jnp.maximum, tops)
        carries = [jnp.exp(t - top) for t in tops]
        total = functools.reduce(jnp.add, [t * c for t, c in zip(totals, carries)])
        result = jnp.zeros((padded, half), jnp.float32)
        for step in range(floors):
            if side + step > 0:
                arrived(home_in.at[places[step]], NUMER, places[step])
            result = result + home_in[places[step]].astype(jnp.float32) * (carries[step] / total)
        out_ref[mine if side == 0 else other, :] = result.T.astype(jnp.bfloat16)[:, :part]
    for copy, only in started:
        if only is None:
            copy.wait_send()
        else:
            pl.when(only)(copy.wait_send)


def plane_body(queries, assign, band_mask, keys, labels, prior):
    clusters = lax.axis_size("cluster")
    floors = clusters // 2
    half, width = queries.shape[0] // 2, queries.shape[1]
    rows, depth = keys.shape
    part = labels.shape[1] // 4
    padded = -(-part // 128) * 128
    vmem = pl.BlockSpec(memory_space=pltpu.VMEM)
    bf16, f32 = jnp.bfloat16, jnp.float32
    copies = 112
    return pl.pallas_call(
        functools.partial(plane_kernel, temper / math.sqrt(depth)),
        out_shape=jax.ShapeDtypeStruct((2 * half, part), bf16),
        in_specs=[pl.BlockSpec(memory_space=pltpu.HBM)] * 6,
        out_specs=vmem,
        scratch_shapes=[
            pltpu.VMEM((1, 2 * half), jnp.int32),
            pltpu.SMEM(band_mask.shape, jnp.int32),
            pltpu.VMEM((1, rows), bf16),
            pltpu.VMEM((4 * part, rows), bf16),
            pltpu.VMEM((floors, 2, 2, half, width), bf16),
            pltpu.VMEM((floors, clusters, half), f32),
            pltpu.VMEM((4 * rows, depth), bf16),
            pltpu.VMEM((4, 2, 2, padded, rows), bf16),
            pltpu.VMEM((4, 8, rows), f32),
            pltpu.VMEM((4 * rows, half), f32),
            pltpu.VMEM((floors, 4 * rows, half), bf16),
            pltpu.VMEM((floors, 8, half), f32),
            pltpu.VMEM((floors, 2, padded, half), bf16),
            pltpu.VMEM((floors, 2, padded, half), bf16),
            pltpu.VMEM((floors, 8, half), f32),
            pltpu.VMEM((floors, 2, padded, half), bf16),
            pltpu.VMEM((floors, 8, half), f32),
            pltpu.VMEM((2 * floors, padded, half), bf16),
            pltpu.VMEM((2 * floors, 8, half), f32),
            pltpu.SemaphoreType.DMA((copies,)),
            pltpu.SemaphoreType.DMA((copies,)),
            pltpu.SemaphoreType.DMA((7, 2 * floors)),
            pltpu.SemaphoreType.DMA((6,)),
        ],
        compiler_params=pltpu.CompilerParams(
            collective_id=0, has_side_effects=True, vmem_limit_bytes=60 * 1024 * 1024
        ),
    )(queries, assign.reshape(1, -1), band_mask, keys, labels.T, prior.reshape(1, -1))


def from_behind(array, axis, by):
    peers = lax.axis_size(axis)
    return lax.ppermute(array, axis, [(i, (i + by) % peers) for i in range(peers)])


def combined_all(part, axis, combine):
    gathered = jax.tree.map(lambda a: lax.all_gather(a, axis), part)

    def take(source):
        return jax.tree.map(lambda a: lax.dynamic_index_in_dim(a, source, 0, False), gathered)

    return lax.fori_loop(
        1, lax.axis_size(axis), lambda source, state: combine(state, take(source)), take(0)
    )


def combine_totals(first, second):
    top_first, sum_first = first
    top_second, sum_second = second
    highest = jnp.maximum(top_first, top_second)
    return (
        highest,
        sum_first * jnp.exp(top_first - highest) + sum_second * jnp.exp(top_second - highest),
    )


def absorb(state, block, query_full, enabled):
    running, total, accum = state
    block_keys, block_labels, block_prior = block
    scale = temper / math.sqrt(query_full.shape[1])
    scores = (
        jnp.einsum("qd,kd->qk", query_full, block_keys, preferred_element_type=jnp.float32) * scale
    )
    scores = scores + block_prior.astype(jnp.float32)[None, :]
    scores = jnp.where(enabled, scores, jnp.float32(-1e30))
    highest = jnp.maximum(running, jnp.max(scores, axis=1))
    carried = jnp.exp(running - highest)
    weight = jnp.exp(scores - highest[:, None])
    total = total * carried + jnp.sum(weight, axis=1)
    accum = accum * carried[:, None] + jnp.dot(
        weight.astype(jnp.bfloat16), block_labels, preferred_element_type=jnp.float32
    )
    return (highest, total, accum)


def body(queries, assign, band_mask, keys, labels, prior):
    clusters = lax.axis_size("cluster")
    cluster_index = lax.axis_index("cluster")
    local_rows = queries.shape[0]
    capacity = 2 * local_rows // clusters
    slots = clusters * capacity
    target = assign[:, 0]
    onehot = (target[:, None] == jnp.arange(clusters, dtype=jnp.int32)[None, :]).astype(jnp.int32)
    before = jnp.cumsum(onehot, axis=0) - onehot
    position = target * capacity + jnp.sum(before * onehot, axis=1)
    outgoing = jnp.zeros((slots, queries.shape[1]), queries.dtype).at[position].set(queries)
    arrived = lax.all_to_all(
        outgoing.reshape(clusters, capacity, queries.shape[1]),
        "cluster",
        split_axis=0,
        concat_axis=0,
        tiled=True,
    )
    query_full = lax.all_gather(
        arrived.reshape(slots, queries.shape[1]), "feat", axis=1, tiled=True
    )
    mask_row = band_mask[cluster_index]
    classes = labels.shape[1]
    state = (
        jnp.full((slots,), -1e30, jnp.float32),
        jnp.zeros((slots,), jnp.float32),
        jnp.zeros((slots, classes), jnp.float32),
    )
    state = absorb(state, (keys, labels, prior), query_full, jnp.bool_(True))

    def visit(current, block, offset):
        enabled = mask_row[REACH + offset] > 0
        return absorb(current, block, query_full, enabled)

    up_keys, up_labels, up_prior = (keys, labels, prior)
    down_keys, down_labels, down_prior = (keys, labels, prior)
    for reach in range(1, REACH + 1):
        up_keys, up_labels, up_prior = from_behind((up_keys, up_labels, up_prior), "cluster", -1)
        state = visit(state, (up_keys, up_labels, up_prior), reach)
        down_keys, down_labels, down_prior = from_behind(
            (down_keys, down_labels, down_prior), "cluster", 1
        )
        state = visit(state, (down_keys, down_labels, down_prior), -reach)
    running, total, accum = state
    highest, grand_total = combined_all((running, total), "feat", combine_totals)
    factor = jnp.exp(running - highest) / grand_total
    shares = lax.psum_scatter(
        (accum * factor[:, None]).astype(jnp.bfloat16), "feat", scatter_dimension=1, tiled=True
    )
    returned = lax.all_to_all(
        shares.reshape(clusters, capacity, shares.shape[1]),
        "cluster",
        split_axis=0,
        concat_axis=0,
        tiled=True,
    )
    return returned.reshape(slots, shares.shape[1])[position]


def solution(mesh):
    in_specs = (
        P("cluster", "feat"),
        P("cluster", None),
        P(),
        P(("cluster", "feat"), None),
        P(("cluster", "feat"), None),
        P(("cluster", "feat")),
    )
    out_specs = P("cluster", "feat")
    planes = mesh.shape["cluster"] == 8 and mesh.shape["feat"] == 4
    return jax.shard_map(plane_body if planes else body, mesh=mesh, in_specs=in_specs, out_specs=out_specs, check_vma=False)
```

```python
import functools
import math

import jax
import jax.numpy as jnp
from jax import lax
from jax.experimental import pallas as pl
from jax.experimental.pallas import tpu as pltpu
from jax.sharding import PartitionSpec as P

REACH = 3
HIDDEN = -1e30
MESH = pl.DeviceIdType.MESH


temper = 2.0


def spread(row, width):
    return jnp.broadcast_to(row, (width, row.shape[1])).T


def plane_kernel(
    scale,
    queries_ref,
    assign_ref,
    mask_ref,
    keys_ref,
    labels_ref,
    prior_ref,
    out_ref,
    assign_buf,
    mask_buf,
    prior_buf,
    labels_buf,
    qbuf,
    vbuf,
    kbuf,
    lbuf,
    pbuf,
    bias,
    weights,
    stats_own,
    numer_out,
    numer_in,
    stats_in,
    home_out,
    home_stats_out,
    home_in,
    home_stats_in,
    send_sem,
    recv_sem,
    home_sem,
    load_sem,
):
    cluster = lax.axis_index("cluster")
    feat = lax.axis_index("feat")
    clusters = mask_ref.shape[0]
    floors = clusters // 2
    half = queries_ref.shape[0] // 2
    rows = keys_ref.shape[0]
    part = labels_ref.shape[0] // 4
    padded = lbuf.shape[3]
    z, y = lax.div(cluster, 2), lax.rem(cluster, 2)
    x, core = lax.div(feat, 2), lax.rem(feat, 2)
    twin = (cluster, feat + 1 - 2 * core)
    across = (cluster, feat + 2 - 4 * x)
    beside = (cluster + 1 - 2 * y, feat)

    def mate(peer):
        return (peer[0], peer[1] + 1 - 2 * core)

    above, below = (cluster + 2, feat), (cluster - 2, feat)
    FIRST, SECOND, ACROSS, ACROSS_SECOND, EXTRA, SEEN, NUMER, STATS = range(8)

    loads = [
        pltpu.make_async_copy(src, dst, load_sem.at[index])
        for index, (src, dst) in enumerate(
            [
                (queries_ref.at[pl.ds(core * half, half)], qbuf.at[z, x, core]),
                (prior_ref, prior_buf),
                (labels_ref, labels_buf),
                (mask_ref, mask_buf),
                (assign_ref, assign_buf),
                (keys_ref, kbuf.at[pl.ds(0, rows)]),
            ]
        )
    ]
    for load in loads:
        load.start()

    inner = jnp.minimum(z, floors - 1 - z)
    upper = lax.div(z, 2)

    def home_at(step):
        if step == 0:
            return z
        near = step - inner if step == 1 else step + 0 * inner
        return near + upper * (floors - 1 - 2 * near)

    homes = [home_at(step) for step in range(floors)]

    def floor_peer(floor):
        return (2 * floor + y, feat)

    barrier = pltpu.get_barrier_semaphore()
    peers = [twin, across, mate(across), beside]
    for home in homes[1:]:
        peers += [floor_peer(home), mate(floor_peer(home))]
    for peer in peers:
        pl.semaphore_signal(barrier, inc=1, device_id=peer, device_id_type=MESH)
    pl.semaphore_wait(barrier, len(peers))

    started = []

    def send(src, dst, peer, where=None, only=None):
        index = len(started)
        copy = pltpu.make_async_remote_copy(
            src_ref=src,
            dst_ref=dst,
            send_sem=send_sem.at[index],
            recv_sem=recv_sem.at[index] if where is None else home_sem.at[where[0], where[1]],
            device_id=peer,
            device_id_type=MESH,
        )
        started.append((copy, only))
        if only is None:
            copy.start()
        else:
            pl.when(only)(copy.start)
        return copy

    def arrived(ref, kind, index, only=None):
        copy = pltpu.make_async_remote_copy(
            src_ref=ref,
            dst_ref=ref,
            send_sem=send_sem.at[0],
            recv_sem=home_sem.at[kind, index],
            device_id=twin,
            device_id_type=MESH,
        )
        if only is None:
            copy.wait_recv()
        else:
            pl.when(only)(copy.wait_recv)

    mine = pl.ds(pl.multiple_of(core * half, half), half)
    other = pl.ds(pl.multiple_of((1 - core) * half, half), half)
    up, down = z < floors - 1, z > 0

    def block(index):
        return pl.ds(index * rows, rows)

    keys_beside = send(keys_ref, kbuf.at[block(2)], beside)
    own, piece = qbuf.at[z, x, core], core
    query_twin = send(queries_ref.at[other], own, twin)
    send(queries_ref.at[mine], own, above, (FIRST + piece, z), up)
    send(queries_ref.at[mine], own, below, (FIRST + piece, z), down)
    send(queries_ref.at[other], own, mate(above), (FIRST + piece, z), up)
    send(queries_ref.at[other], own, mate(below), (FIRST + piece, z), down)
    send(queries_ref.at[mine], own, across, (FIRST + piece, z))
    send(queries_ref.at[other], own, mate(across), (FIRST + piece, z))
    keys_twin = send(keys_ref, kbuf.at[block(1)], twin)
    loads[1].wait()
    pbuf[0] = jnp.broadcast_to(prior_buf[...].astype(jnp.float32), (8, rows))
    prior_beside = send(pbuf.at[0], pbuf.at[2], beside)
    prior_twin = send(pbuf.at[0], pbuf.at[1], twin)

    def pass_on(home, kind, ref, only):
        send(ref, ref, above, (kind, home), only & (home <= z) & up)
        send(ref, ref, below, (kind, home), only & (home >= z) & down)

    lbuf[0] = jnp.zeros(lbuf.shape[1:], lbuf.dtype)
    loads[2].wait()
    for quarter in range(4):
        lbuf[0, quarter // 2, quarter % 2, :part, :] = labels_buf[
            quarter * part : (quarter + 1) * part, :
        ]
    quarters = [(1 - x, 0), (1 - x, 1), (x, 0), (x, 1)]
    labels_beside, labels_twin, labels_relay = [], [], []
    for side, turn in quarters:
        labels_beside.append(send(lbuf.at[0, side, turn], lbuf.at[2, side, turn], beside))
        labels_twin.append(send(lbuf.at[0, side, turn], lbuf.at[1, side, turn], twin))

    def relay_labels(index):
        side, turn = quarters[index]
        labels_beside[index].wait_recv()
        labels_relay.append(send(lbuf.at[2, side, turn], lbuf.at[3, side, turn], twin))

    def labels_here(index):
        labels_twin[index].wait_recv()
        labels_relay[index].wait_recv()

    loads[3].wait()
    loads[4].wait()
    assigned = assign_buf[...]
    assigned = jnp.where(core == 0, assigned[:, :half], assigned[:, half:])
    assigned = jnp.broadcast_to(assigned, (clusters, half))
    row = lax.broadcasted_iota(jnp.int32, (clusters, half), 0)
    seen = jnp.zeros((clusters, half), jnp.int32)
    for owner in range(clusters):
        column = jnp.zeros((clusters, half), jnp.int32)
        for step in range(2 * REACH + 1):
            column = jnp.where(
                row == (owner + step - REACH) % clusters, mask_buf[owner, step], column
            )
        seen = jnp.where(assigned == owner, column, seen)
    vbuf[z] = jnp.where(seen > 0, jnp.float32(0.0), jnp.float32(HIDDEN))
    for home in homes[1:]:
        send(vbuf.at[z], vbuf.at[z], floor_peer(home), (SEEN, z))

    early, late = pl.ds(0, half // 2), pl.ds(half // 2, half // 2)

    def relay(step, only):
        home = homes[step]
        for turn, (kind, copied) in enumerate(((FIRST, ACROSS), (SECOND, ACROSS_SECOND))):
            part_here = qbuf.at[home, x, turn]
            arrived(part_here, kind, home, only)
            pass_on(home, kind, part_here, only)
            if turn == 1:
                part_here = part_here.at[late]
            send(part_here, part_here, across, (copied, home), only)

    def extra_piece(home):
        return qbuf.at[home, 1 - x, 1, early]

    def relay_extra(step, only):
        arrived(extra_piece(homes[step]), EXTRA, homes[step], only)
        pass_on(homes[step], EXTRA, extra_piece(homes[step]), only)

    def score(step):
        home = homes[step]
        if step > 0:
            arrived(qbuf.at[home, 1 - x, 0], ACROSS, home)
            arrived(qbuf.at[home, 1 - x, 1, late], ACROSS_SECOND, home)
            arrived(vbuf.at[home], SEEN, home)
        features = jnp.concatenate(
            [qbuf[home, quarter // 2, quarter % 2] for quarter in range(4)], axis=1
        )
        scores = scale * lax.dot_general(
            kbuf[...], features, (((1,), (1,)), ((), ())), preferred_element_type=jnp.float32
        )
        near = vbuf[home, pl.ds(cluster, 1), :]
        far = vbuf[home, pl.ds(cluster + 1 - 2 * y, 1), :]
        pieces = []
        for index in range(4):
            cut = slice(index * rows, (index + 1) * rows)
            pieces.append(scores[cut] + bias[cut, :] + (near if index < 2 else far))
        scores = jnp.concatenate(pieces, axis=0)
        top = jnp.max(scores, axis=0, keepdims=True)
        weight = jnp.exp(scores - top)
        total = jnp.sum(weight, axis=0, keepdims=True)
        weights[step] = weight.astype(jnp.bfloat16)
        stats_own[step, 0:1, :] = top
        stats_own[step, 1:2, :] = total
        stats_own[step, 2:8, :] = jnp.zeros((6, half), jnp.float32)

    def class_sum(step, side, turn):
        blocks = jnp.concatenate([lbuf[index, side, turn] for index in range(4)], axis=1)
        return jnp.dot(blocks, weights[step], preferred_element_type=jnp.float32)

    numer_across, stats_across, carried = {}, {}, {}

    def send_across(step, turn):
        numer_out[step, turn] = class_sum(step, 1 - x, turn).astype(jnp.bfloat16)
        if turn == 0:
            stats_across[step] = send(stats_own.at[step], stats_in.at[step], across)
        numer_across[step, turn] = send(
            numer_out.at[step, turn], numer_in.at[step, turn], across
        )

    place = 2 * z + core

    def merge(step, turn):
        numer = class_sum(step, x, turn)
        floor = homes[step]
        if turn == 0:
            stats_across[step].wait_recv()
            top_own, top_in = stats_own[step, 0:1, :], stats_in[step, 0:1, :]
            top = jnp.maximum(top_own, top_in)
            carry_own, carry_in = jnp.exp(top_own - top), jnp.exp(top_in - top)
            total = stats_own[step, 1:2, :] * carry_own + stats_in[step, 1:2, :] * carry_in
            carried[step] = carry_own, carry_in
            home_stats_out[step, 0:1, :] = top
            home_stats_out[step, 1:2, :] = total
            home_stats_out[step, 2:8, :] = jnp.zeros((6, half), jnp.float32)
            if step > 0:
                for peer in (floor_peer(floor), mate(floor_peer(floor))):
                    send(home_stats_out.at[step], home_stats_in.at[place], peer, (STATS, place))
            else:
                home_stats_in[place] = home_stats_out[0]
                send(home_stats_out.at[0], home_stats_in.at[place], twin, (STATS, place))
        carry_own, carry_in = carried[step]
        numer_across[step, turn].wait_recv()
        merged = numer * carry_own + numer_in[step, turn].astype(jnp.float32) * carry_in
        home_out[step, turn] = merged.astype(jnp.bfloat16)
        if step > 0:
            peer = (2 * floor + y, 2 * x + turn)
            send(home_out.at[step, turn], home_in.at[place], peer, (NUMER, place))
        elif turn == 1:
            home_in[place] = home_out[0, core]
            send(home_out.at[0, 1 - core], home_in.at[place], twin, (NUMER, place))

    always, inside, at_end = z >= 0, inner > 0, inner == 0
    relay(1, always)
    arrived(qbuf.at[z, 1 - x, 0], FIRST, z)
    arrived(qbuf.at[z, 1 - x, 1], SECOND, z)
    pass_on(z, EXTRA, extra_piece(z), always)
    relay(2, inside)
    keys_beside.wait_recv()
    prior_beside.wait_recv()
    keys_relay = send(kbuf.at[block(2)], kbuf.at[block(3)], twin)
    prior_relay = send(pbuf.at[2], pbuf.at[3], twin)
    relay_extra(1, always)
    relay_extra(2, inside)
    relay(3, inside)
    relay_extra(3, inside)
    relay(2, at_end)
    for copy in (keys_twin, prior_twin, keys_relay, prior_relay, query_twin):
        copy.wait_recv()
    loads[0].wait()
    loads[5].wait()
    for index in range(4):
        bias[block(index), :] = spread(pbuf[index, 0:1, :], half)
    score(0)
    score(1)
    relay_labels(0)
    relay_extra(2, at_end)
    score(2)
    labels_here(0)
    send_across(2, 0)
    relay_labels(1)
    relay(3, at_end)
    relay_extra(3, at_end)
    labels_here(1)
    send_across(2, 1)
    score(3)
    send_across(3, 0)
    send_across(3, 1)
    relay_labels(2)
    send_across(1, 0)
    send_across(1, 1)
    labels_here(2)
    merge(2, 0)
    relay_labels(3)
    labels_here(3)
    merge(2, 1)
    merge(3, 0)
    send_across(0, 0)
    send_across(0, 1)
    merge(3, 1)
    for step in (1, 0):
        merge(step, 0)
        merge(step, 1)

    for side in (0, 1):
        source = core if side == 0 else 1 - core
        places = [2 * home + source for home in homes]
        for step in range(floors):
            if side + step > 0:
                arrived(home_stats_in.at[places[step]], STATS, places[step])
        tops = [home_stats_in[place, 0:1, :] for place in places]
        totals = [home_stats_in[place, 1:2, :] for place in places]
        top = functools.reduce(jnp.maximum, tops)
        carries = [jnp.exp(t - top) for t in tops]
        total = functools.reduce(jnp.add, [t * c for t, c in zip(totals, carries)])
        result = jnp.zeros((padded, half), jnp.float32)
        for step in range(floors):
            if side + step > 0:
                arrived(home_in.at[places[step]], NUMER, places[step])
            result = result + home_in[places[step]].astype(jnp.float32) * (carries[step] / total)
        out_ref[mine if side == 0 else other, :] = result.T.astype(jnp.bfloat16)[:, :part]
    for copy, only in started:
        if only is None:
            copy.wait_send()
        else:
            pl.when(only)(copy.wait_send)


def plane_body(queries, assign, band_mask, keys, labels, prior):
    clusters = lax.axis_size("cluster")
    floors = clusters // 2
    half, width = queries.shape[0] // 2, queries.shape[1]
    rows, depth = keys.shape
    part = labels.shape[1] // 4
    padded = -(-part // 128) * 128
    vmem = pl.BlockSpec(memory_space=pltpu.VMEM)
    bf16, f32 = jnp.bfloat16, jnp.float32
    copies = 112
    return pl.pallas_call(
        functools.partial(plane_kernel, temper / math.sqrt(depth)),
        out_shape=jax.ShapeDtypeStruct((2 * half, part), bf16),
        in_specs=[pl.BlockSpec(memory_space=pltpu.HBM)] * 6,
        out_specs=vmem,
        scratch_shapes=[
            pltpu.VMEM((1, 2 * half), jnp.int32),
            pltpu.SMEM(band_mask.shape, jnp.int32),
            pltpu.VMEM((1, rows), bf16),
            pltpu.VMEM((4 * part, rows), bf16),
            pltpu.VMEM((floors, 2, 2, half, width), bf16),
            pltpu.VMEM((floors, clusters, half), f32),
            pltpu.VMEM((4 * rows, depth), bf16),
            pltpu.VMEM((4, 2, 2, padded, rows), bf16),
            pltpu.VMEM((4, 8, rows), f32),
            pltpu.VMEM((4 * rows, half), f32),
            pltpu.VMEM((floors, 4 * rows, half), bf16),
            pltpu.VMEM((floors, 8, half), f32),
            pltpu.VMEM((floors, 2, padded, half), bf16),
            pltpu.VMEM((floors, 2, padded, half), bf16),
            pltpu.VMEM((floors, 8, half), f32),
            pltpu.VMEM((floors, 2, padded, half), bf16),
            pltpu.VMEM((floors, 8, half), f32),
            pltpu.VMEM((2 * floors, padded, half), bf16),
            pltpu.VMEM((2 * floors, 8, half), f32),
            pltpu.SemaphoreType.DMA((copies,)),
            pltpu.SemaphoreType.DMA((copies,)),
            pltpu.SemaphoreType.DMA((8, 2 * floors)),
            pltpu.SemaphoreType.DMA((6,)),
        ],
        compiler_params=pltpu.CompilerParams(
            collective_id=0, has_side_effects=True, vmem_limit_bytes=60 * 1024 * 1024
        ),
    )(queries, assign.reshape(1, -1), band_mask, keys, labels.T, prior.reshape(1, -1))


def from_behind(array, axis, by):
    peers = lax.axis_size(axis)
    return lax.ppermute(array, axis, [(i, (i + by) % peers) for i in range(peers)])


def combined_all(part, axis, combine):
    gathered = jax.tree.map(lambda a: lax.all_gather(a, axis), part)

    def take(source):
        return jax.tree.map(lambda a: lax.dynamic_index_in_dim(a, source, 0, False), gathered)

    return lax.fori_loop(
        1, lax.axis_size(axis), lambda source, state: combine(state, take(source)), take(0)
    )


def combine_totals(first, second):
    top_first, sum_first = first
    top_second, sum_second = second
    highest = jnp.maximum(top_first, top_second)
    return (
        highest,
        sum_first * jnp.exp(top_first - highest) + sum_second * jnp.exp(top_second - highest),
    )


def absorb(state, block, query_full, enabled):
    running, total, accum = state
    block_keys, block_labels, block_prior = block
    scale = temper / math.sqrt(query_full.shape[1])
    scores = (
        jnp.einsum("qd,kd->qk", query_full, block_keys, preferred_element_type=jnp.float32) * scale
    )
    scores = scores + block_prior.astype(jnp.float32)[None, :]
    scores = jnp.where(enabled, scores, jnp.float32(-1e30))
    highest = jnp.maximum(running, jnp.max(scores, axis=1))
    carried = jnp.exp(running - highest)
    weight = jnp.exp(scores - highest[:, None])
    total = total * carried + jnp.sum(weight, axis=1)
    accum = accum * carried[:, None] + jnp.dot(
        weight.astype(jnp.bfloat16), block_labels, preferred_element_type=jnp.float32
    )
    return (highest, total, accum)


def body(queries, assign, band_mask, keys, labels, prior):
    clusters = lax.axis_size("cluster")
    cluster_index = lax.axis_index("cluster")
    local_rows = queries.shape[0]
    capacity = 2 * local_rows // clusters
    slots = clusters * capacity
    target = assign[:, 0]
    onehot = (target[:, None] == jnp.arange(clusters, dtype=jnp.int32)[None, :]).astype(jnp.int32)
    before = jnp.cumsum(onehot, axis=0) - onehot
    position = target * capacity + jnp.sum(before * onehot, axis=1)
    outgoing = jnp.zeros((slots, queries.shape[1]), queries.dtype).at[position].set(queries)
    arrived = lax.all_to_all(
        outgoing.reshape(clusters, capacity, queries.shape[1]),
        "cluster",
        split_axis=0,
        concat_axis=0,
        tiled=True,
    )
    query_full = lax.all_gather(
        arrived.reshape(slots, queries.shape[1]), "feat", axis=1, tiled=True
    )
    mask_row = band_mask[cluster_index]
    classes = labels.shape[1]
    state = (
        jnp.full((slots,), -1e30, jnp.float32),
        jnp.zeros((slots,), jnp.float32),
        jnp.zeros((slots, classes), jnp.float32),
    )
    state = absorb(state, (keys, labels, prior), query_full, jnp.bool_(True))

    def visit(current, block, offset):
        enabled = mask_row[REACH + offset] > 0
        return absorb(current, block, query_full, enabled)

    up_keys, up_labels, up_prior = (keys, labels, prior)
    down_keys, down_labels, down_prior = (keys, labels, prior)
    for reach in range(1, REACH + 1):
        up_keys, up_labels, up_prior = from_behind((up_keys, up_labels, up_prior), "cluster", -1)
        state = visit(state, (up_keys, up_labels, up_prior), reach)
        down_keys, down_labels, down_prior = from_behind(
            (down_keys, down_labels, down_prior), "cluster", 1
        )
        state = visit(state, (down_keys, down_labels, down_prior), -reach)
    running, total, accum = state
    highest, grand_total = combined_all((running, total), "feat", combine_totals)
    factor = jnp.exp(running - highest) / grand_total
    shares = lax.psum_scatter(
        (accum * factor[:, None]).astype(jnp.bfloat16), "feat", scatter_dimension=1, tiled=True
    )
    returned = lax.all_to_all(
        shares.reshape(clusters, capacity, shares.shape[1]),
        "cluster",
        split_axis=0,
        concat_axis=0,
        tiled=True,
    )
    return returned.reshape(slots, shares.shape[1])[position]


def solution(mesh):
    in_specs = (
        P("cluster", "feat"),
        P("cluster", None),
        P(),
        P(("cluster", "feat"), None),
        P(("cluster", "feat"), None),
        P(("cluster", "feat")),
    )
    out_specs = P("cluster", "feat")
    planes = mesh.shape["cluster"] == 8 and mesh.shape["feat"] == 4
    return jax.shard_map(plane_body if planes else body, mesh=mesh, in_specs=in_specs, out_specs=out_specs, check_vma=False)
```

```python
import functools
import math

import jax
import jax.numpy as jnp
from jax import lax
from jax.experimental import pallas as pl
from jax.experimental.pallas import tpu as pltpu
from jax.sharding import PartitionSpec as P

REACH = 3
HIDDEN = -1e30
MESH = pl.DeviceIdType.MESH


temper = 2.0


def spread(row, width):
    return jnp.broadcast_to(row, (width, row.shape[1])).T


def plane_kernel(
    scale,
    queries_ref,
    assign_ref,
    mask_ref,
    keys_ref,
    labels_ref,
    prior_ref,
    out_ref,
    assign_buf,
    mask_buf,
    prior_buf,
    labels_buf,
    qbuf,
    vbuf,
    kbuf,
    lbuf,
    pbuf,
    bias,
    weights,
    stats_own,
    numer_out,
    numer_in,
    stats_in,
    home_out,
    home_stats_out,
    home_in,
    home_stats_in,
    send_sem,
    recv_sem,
    home_sem,
    load_sem,
):
    cluster = lax.axis_index("cluster")
    feat = lax.axis_index("feat")
    clusters = mask_ref.shape[0]
    floors = clusters // 2
    half = queries_ref.shape[0] // 2
    rows = keys_ref.shape[0]
    part = labels_ref.shape[0] // 4
    padded = lbuf.shape[3]
    z, y = lax.div(cluster, 2), lax.rem(cluster, 2)
    x, core = lax.div(feat, 2), lax.rem(feat, 2)
    twin = (cluster, feat + 1 - 2 * core)
    across = (cluster, feat + 2 - 4 * x)
    beside = (cluster + 1 - 2 * y, feat)

    def mate(peer):
        return (peer[0], peer[1] + 1 - 2 * core)

    above, below = (cluster + 2, feat), (cluster - 2, feat)
    FIRST, SECOND, ACROSS, ACROSS_SECOND, EXTRA, SEEN, NUMER, STATS = range(8)

    loads = [
        pltpu.make_async_copy(src, dst, load_sem.at[index])
        for index, (src, dst) in enumerate(
            [
                (queries_ref.at[pl.ds(core * half, half)], qbuf.at[z, x, core]),
                (prior_ref, prior_buf),
                (labels_ref, labels_buf),
                (mask_ref, mask_buf),
                (assign_ref, assign_buf),
                (keys_ref, kbuf.at[pl.ds(0, rows)]),
            ]
        )
    ]
    for load in loads:
        load.start()

    inner = jnp.minimum(z, floors - 1 - z)
    upper = lax.div(z, 2)

    def home_at(step):
        if step == 0:
            return z
        near = step - inner if step == 1 else step + 0 * inner
        return near + upper * (floors - 1 - 2 * near)

    homes = [home_at(step) for step in range(floors)]

    def floor_peer(floor):
        return (2 * floor + y, feat)

    barrier = pltpu.get_barrier_semaphore()
    peers = [twin, across, mate(across), beside]
    for home in homes[1:]:
        peers += [floor_peer(home), mate(floor_peer(home))]
    for peer in peers:
        pl.semaphore_signal(barrier, inc=1, device_id=peer, device_id_type=MESH)
    pl.semaphore_wait(barrier, len(peers))

    started = []

    def send(src, dst, peer, where=None, only=None):
        index = len(started)
        copy = pltpu.make_async_remote_copy(
            src_ref=src,
            dst_ref=dst,
            send_sem=send_sem.at[index],
            recv_sem=recv_sem.at[index] if where is None else home_sem.at[where[0], where[1]],
            device_id=peer,
            device_id_type=MESH,
        )
        started.append((copy, only))
        if only is None:
            copy.start()
        else:
            pl.when(only)(copy.start)
        return copy

    def arrived(ref, kind, index, only=None):
        copy = pltpu.make_async_remote_copy(
            src_ref=ref,
            dst_ref=ref,
            send_sem=send_sem.at[0],
            recv_sem=home_sem.at[kind, index],
            device_id=twin,
            device_id_type=MESH,
        )
        if only is None:
            copy.wait_recv()
        else:
            pl.when(only)(copy.wait_recv)

    mine = pl.ds(pl.multiple_of(core * half, half), half)
    other = pl.ds(pl.multiple_of((1 - core) * half, half), half)
    up, down = z < floors - 1, z > 0

    def block(index):
        return pl.ds(index * rows, rows)

    keys_beside = send(keys_ref, kbuf.at[block(2)], beside)
    own, piece = qbuf.at[z, x, core], core
    query_twin = send(queries_ref.at[other], own, twin)
    send(queries_ref.at[mine], own, above, (FIRST + piece, z), up)
    send(queries_ref.at[mine], own, below, (FIRST + piece, z), down)
    send(queries_ref.at[other], own, mate(above), (FIRST + piece, z), up)
    send(queries_ref.at[other], own, mate(below), (FIRST + piece, z), down)
    send(queries_ref.at[mine], own, across, (FIRST + piece, z))
    send(queries_ref.at[other], own, mate(across), (FIRST + piece, z))
    keys_twin = send(keys_ref, kbuf.at[block(1)], twin)
    loads[1].wait()
    pbuf[0] = jnp.broadcast_to(prior_buf[...].astype(jnp.float32), (8, rows))
    prior_beside = send(pbuf.at[0], pbuf.at[2], beside)
    prior_twin = send(pbuf.at[0], pbuf.at[1], twin)

    def pass_on(home, kind, ref, only):
        send(ref, ref, above, (kind, home), only & (home <= z) & up)
        send(ref, ref, below, (kind, home), only & (home >= z) & down)

    lbuf[0] = jnp.zeros(lbuf.shape[1:], lbuf.dtype)
    loads[2].wait()
    for quarter in range(4):
        lbuf[0, quarter // 2, quarter % 2, :part, :] = labels_buf[
            quarter * part : (quarter + 1) * part, :
        ]
    quarters = [(1 - x, 0), (1 - x, 1), (x, 0), (x, 1)]
    labels_beside, labels_twin, labels_relay = [], [], []
    for side, turn in quarters:
        labels_beside.append(send(lbuf.at[0, side, turn], lbuf.at[2, side, turn], beside))
        labels_twin.append(send(lbuf.at[0, side, turn], lbuf.at[1, side, turn], twin))

    def relay_labels(index):
        side, turn = quarters[index]
        labels_beside[index].wait_recv()
        labels_relay.append(send(lbuf.at[2, side, turn], lbuf.at[3, side, turn], twin))

    def labels_here(index):
        labels_twin[index].wait_recv()
        labels_relay[index].wait_recv()

    loads[3].wait()
    loads[4].wait()
    assigned = assign_buf[...]
    assigned = jnp.where(core == 0, assigned[:, :half], assigned[:, half:])
    assigned = jnp.broadcast_to(assigned, (clusters, half))
    row = lax.broadcasted_iota(jnp.int32, (clusters, half), 0)
    seen = jnp.zeros((clusters, half), jnp.int32)
    for owner in range(clusters):
        column = jnp.zeros((clusters, half), jnp.int32)
        for step in range(2 * REACH + 1):
            column = jnp.where(
                row == (owner + step - REACH) % clusters, mask_buf[owner, step], column
            )
        seen = jnp.where(assigned == owner, column, seen)
    vbuf[z] = jnp.where(seen > 0, jnp.float32(0.0), jnp.float32(HIDDEN))
    for home in homes[1:]:
        send(vbuf.at[z], vbuf.at[z], floor_peer(home), (SEEN, z))

    early, late = pl.ds(0, half // 2), pl.ds(half // 2, half // 2)

    def relay(step, only):
        home = homes[step]
        for turn, (kind, copied) in enumerate(((FIRST, ACROSS), (SECOND, ACROSS_SECOND))):
            part_here = qbuf.at[home, x, turn]
            arrived(part_here, kind, home, only)
            pass_on(home, kind, part_here, only)
            if turn == 1:
                part_here = part_here.at[late]
            send(part_here, part_here, across, (copied, home), only)

    def extra_piece(home):
        return qbuf.at[home, 1 - x, 1, early]

    def relay_extra(step, only):
        arrived(extra_piece(homes[step]), EXTRA, homes[step], only)
        pass_on(homes[step], EXTRA, extra_piece(homes[step]), only)

    def score(step):
        home = homes[step]
        if step > 0:
            arrived(qbuf.at[home, 1 - x, 0], ACROSS, home)
            arrived(qbuf.at[home, 1 - x, 1, late], ACROSS_SECOND, home)
            arrived(vbuf.at[home], SEEN, home)
        features = jnp.concatenate(
            [qbuf[home, quarter // 2, quarter % 2] for quarter in range(4)], axis=1
        )
        scores = scale * lax.dot_general(
            kbuf[...], features, (((1,), (1,)), ((), ())), preferred_element_type=jnp.float32
        )
        near = vbuf[home, pl.ds(cluster, 1), :]
        far = vbuf[home, pl.ds(cluster + 1 - 2 * y, 1), :]
        pieces = []
        for index in range(4):
            cut = slice(index * rows, (index + 1) * rows)
            pieces.append(scores[cut] + bias[cut, :] + (near if index < 2 else far))
        scores = jnp.concatenate(pieces, axis=0)
        top = jnp.max(scores, axis=0, keepdims=True)
        weight = jnp.exp(scores - top)
        total = jnp.sum(weight, axis=0, keepdims=True)
        weights[step] = weight.astype(jnp.bfloat16)
        stats_own[step, 0:1, :] = top
        stats_own[step, 1:2, :] = total
        stats_own[step, 2:8, :] = jnp.zeros((6, half), jnp.float32)

    def class_sum(step, side, turn):
        blocks = jnp.concatenate([lbuf[index, side, turn] for index in range(4)], axis=1)
        return jnp.dot(blocks, weights[step], preferred_element_type=jnp.float32)

    numer_across, stats_across, carried = {}, {}, {}

    def send_across(step, turn):
        numer_out[step, turn] = class_sum(step, 1 - x, turn).astype(jnp.bfloat16)
        if turn == 0:
            stats_across[step] = send(stats_own.at[step], stats_in.at[step], across)
        numer_across[step, turn] = send(
            numer_out.at[step, turn], numer_in.at[step, turn], across
        )

    place = 2 * z + core

    def merge(step, turn):
        numer = class_sum(step, x, turn)
        floor = homes[step]
        if turn == 0:
            stats_across[step].wait_recv()
            top_own, top_in = stats_own[step, 0:1, :], stats_in[step, 0:1, :]
            top = jnp.maximum(top_own, top_in)
            carry_own, carry_in = jnp.exp(top_own - top), jnp.exp(top_in - top)
            total = stats_own[step, 1:2, :] * carry_own + stats_in[step, 1:2, :] * carry_in
            carried[step] = carry_own, carry_in
            home_stats_out[step, 0:1, :] = top
            home_stats_out[step, 1:2, :] = total
            home_stats_out[step, 2:8, :] = jnp.zeros((6, half), jnp.float32)
            if step > 0:
                for peer in (floor_peer(floor), mate(floor_peer(floor))):
                    send(home_stats_out.at[step], home_stats_in.at[place], peer, (STATS, place))
            else:
                home_stats_in[place] = home_stats_out[0]
                send(home_stats_out.at[0], home_stats_in.at[place], twin, (STATS, place))
        carry_own, carry_in = carried[step]
        numer_across[step, turn].wait_recv()
        merged = numer * carry_own + numer_in[step, turn].astype(jnp.float32) * carry_in
        home_out[step, turn] = merged.astype(jnp.bfloat16)
        if step > 0:
            peer = (2 * floor + y, 2 * x + turn)
            send(home_out.at[step, turn], home_in.at[place], peer, (NUMER, place))
        elif turn == 1:
            home_in[place] = home_out[0, core]
            send(home_out.at[0, 1 - core], home_in.at[place], twin, (NUMER, place))

    always, inside, at_end = z >= 0, inner > 0, inner == 0
    relay(1, always)
    arrived(qbuf.at[z, 1 - x, 0], FIRST, z)
    arrived(qbuf.at[z, 1 - x, 1], SECOND, z)
    pass_on(z, EXTRA, extra_piece(z), always)
    relay(2, inside)
    keys_beside.wait_recv()
    prior_beside.wait_recv()
    keys_relay = send(kbuf.at[block(2)], kbuf.at[block(3)], twin)
    prior_relay = send(pbuf.at[2], pbuf.at[3], twin)
    relay_extra(1, always)
    relay_extra(2, inside)
    relay(3, inside)
    relay_extra(3, inside)
    relay(2, at_end)
    for copy in (keys_twin, prior_twin, keys_relay, prior_relay, query_twin):
        copy.wait_recv()
    loads[0].wait()
    loads[5].wait()
    for index in range(4):
        bias[block(index), :] = spread(pbuf[index, 0:1, :], half)
    score(0)
    score(1)
    relay_labels(0)
    relay_extra(2, at_end)
    score(2)
    labels_here(0)
    send_across(2, 0)
    relay_labels(1)
    labels_here(1)
    send_across(2, 1)
    relay(3, at_end)
    relay_extra(3, at_end)
    score(3)
    send_across(3, 0)
    send_across(3, 1)
    relay_labels(2)
    send_across(1, 0)
    send_across(1, 1)
    labels_here(2)
    merge(2, 0)
    relay_labels(3)
    labels_here(3)
    merge(2, 1)
    merge(3, 0)
    send_across(0, 0)
    send_across(0, 1)
    merge(3, 1)
    for step in (1, 0):
        merge(step, 0)
        merge(step, 1)

    for side in (0, 1):
        source = core if side == 0 else 1 - core
        places = [2 * home + source for home in homes]
        for step in range(floors):
            if side + step > 0:
                arrived(home_stats_in.at[places[step]], STATS, places[step])
        tops = [home_stats_in[place, 0:1, :] for place in places]
        totals = [home_stats_in[place, 1:2, :] for place in places]
        top = functools.reduce(jnp.maximum, tops)
        carries = [jnp.exp(t - top) for t in tops]
        total = functools.reduce(jnp.add, [t * c for t, c in zip(totals, carries)])
        result = jnp.zeros((padded, half), jnp.float32)
        for step in range(floors):
            if side + step > 0:
                arrived(home_in.at[places[step]], NUMER, places[step])
            result = result + home_in[places[step]].astype(jnp.float32) * (carries[step] / total)
        out_ref[mine if side == 0 else other, :] = result.T.astype(jnp.bfloat16)[:, :part]
    for copy, only in started:
        if only is None:
            copy.wait_send()
        else:
            pl.when(only)(copy.wait_send)


def plane_body(queries, assign, band_mask, keys, labels, prior):
    clusters = lax.axis_size("cluster")
    floors = clusters // 2
    half, width = queries.shape[0] // 2, queries.shape[1]
    rows, depth = keys.shape
    part = labels.shape[1] // 4
    padded = -(-part // 128) * 128
    vmem = pl.BlockSpec(memory_space=pltpu.VMEM)
    bf16, f32 = jnp.bfloat16, jnp.float32
    copies = 112
    return pl.pallas_call(
        functools.partial(plane_kernel, temper / math.sqrt(depth)),
        out_shape=jax.ShapeDtypeStruct((2 * half, part), bf16),
        in_specs=[pl.BlockSpec(memory_space=pltpu.HBM)] * 6,
        out_specs=vmem,
        scratch_shapes=[
            pltpu.VMEM((1, 2 * half), jnp.int32),
            pltpu.SMEM(band_mask.shape, jnp.int32),
            pltpu.VMEM((1, rows), bf16),
            pltpu.VMEM((4 * part, rows), bf16),
            pltpu.VMEM((floors, 2, 2, half, width), bf16),
            pltpu.VMEM((floors, clusters, half), f32),
            pltpu.VMEM((4 * rows, depth), bf16),
            pltpu.VMEM((4, 2, 2, padded, rows), bf16),
            pltpu.VMEM((4, 8, rows), f32),
            pltpu.VMEM((4 * rows, half), f32),
            pltpu.VMEM((floors, 4 * rows, half), bf16),
            pltpu.VMEM((floors, 8, half), f32),
            pltpu.VMEM((floors, 2, padded, half), bf16),
            pltpu.VMEM((floors, 2, padded, half), bf16),
            pltpu.VMEM((floors, 8, half), f32),
            pltpu.VMEM((floors, 2, padded, half), bf16),
            pltpu.VMEM((floors, 8, half), f32),
            pltpu.VMEM((2 * floors, padded, half), bf16),
            pltpu.VMEM((2 * floors, 8, half), f32),
            pltpu.SemaphoreType.DMA((copies,)),
            pltpu.SemaphoreType.DMA((copies,)),
            pltpu.SemaphoreType.DMA((8, 2 * floors)),
            pltpu.SemaphoreType.DMA((6,)),
        ],
        compiler_params=pltpu.CompilerParams(
            collective_id=0, has_side_effects=True, vmem_limit_bytes=60 * 1024 * 1024
        ),
    )(queries, assign.reshape(1, -1), band_mask, keys, labels.T, prior.reshape(1, -1))


def from_behind(array, axis, by):
    peers = lax.axis_size(axis)
    return lax.ppermute(array, axis, [(i, (i + by) % peers) for i in range(peers)])


def combined_all(part, axis, combine):
    gathered = jax.tree.map(lambda a: lax.all_gather(a, axis), part)

    def take(source):
        return jax.tree.map(lambda a: lax.dynamic_index_in_dim(a, source, 0, False), gathered)

    return lax.fori_loop(
        1, lax.axis_size(axis), lambda source, state: combine(state, take(source)), take(0)
    )


def combine_totals(first, second):
    top_first, sum_first = first
    top_second, sum_second = second
    highest = jnp.maximum(top_first, top_second)
    return (
        highest,
        sum_first * jnp.exp(top_first - highest) + sum_second * jnp.exp(top_second - highest),
    )


def absorb(state, block, query_full, enabled):
    running, total, accum = state
    block_keys, block_labels, block_prior = block
    scale = temper / math.sqrt(query_full.shape[1])
    scores = (
        jnp.einsum("qd,kd->qk", query_full, block_keys, preferred_element_type=jnp.float32) * scale
    )
    scores = scores + block_prior.astype(jnp.float32)[None, :]
    scores = jnp.where(enabled, scores, jnp.float32(-1e30))
    highest = jnp.maximum(running, jnp.max(scores, axis=1))
    carried = jnp.exp(running - highest)
    weight = jnp.exp(scores - highest[:, None])
    total = total * carried + jnp.sum(weight, axis=1)
    accum = accum * carried[:, None] + jnp.dot(
        weight.astype(jnp.bfloat16), block_labels, preferred_element_type=jnp.float32
    )
    return (highest, total, accum)


def body(queries, assign, band_mask, keys, labels, prior):
    clusters = lax.axis_size("cluster")
    cluster_index = lax.axis_index("cluster")
    local_rows = queries.shape[0]
    capacity = 2 * local_rows // clusters
    slots = clusters * capacity
    target = assign[:, 0]
    onehot = (target[:, None] == jnp.arange(clusters, dtype=jnp.int32)[None, :]).astype(jnp.int32)
    before = jnp.cumsum(onehot, axis=0) - onehot
    position = target * capacity + jnp.sum(before * onehot, axis=1)
    outgoing = jnp.zeros((slots, queries.shape[1]), queries.dtype).at[position].set(queries)
    arrived = lax.all_to_all(
        outgoing.reshape(clusters, capacity, queries.shape[1]),
        "cluster",
        split_axis=0,
        concat_axis=0,
        tiled=True,
    )
    query_full = lax.all_gather(
        arrived.reshape(slots, queries.shape[1]), "feat", axis=1, tiled=True
    )
    mask_row = band_mask[cluster_index]
    classes = labels.shape[1]
    state = (
        jnp.full((slots,), -1e30, jnp.float32),
        jnp.zeros((slots,), jnp.float32),
        jnp.zeros((slots, classes), jnp.float32),
    )
    state = absorb(state, (keys, labels, prior), query_full, jnp.bool_(True))

    def visit(current, block, offset):
        enabled = mask_row[REACH + offset] > 0
        return absorb(current, block, query_full, enabled)

    up_keys, up_labels, up_prior = (keys, labels, prior)
    down_keys, down_labels, down_prior = (keys, labels, prior)
    for reach in range(1, REACH + 1):
        up_keys, up_labels, up_prior = from_behind((up_keys, up_labels, up_prior), "cluster", -1)
        state = visit(state, (up_keys, up_labels, up_prior), reach)
        down_keys, down_labels, down_prior = from_behind(
            (down_keys, down_labels, down_prior), "cluster", 1
        )
        state = visit(state, (down_keys, down_labels, down_prior), -reach)
    running, total, accum = state
    highest, grand_total = combined_all((running, total), "feat", combine_totals)
    factor = jnp.exp(running - highest) / grand_total
    shares = lax.psum_scatter(
        (accum * factor[:, None]).astype(jnp.bfloat16), "feat", scatter_dimension=1, tiled=True
    )
    returned = lax.all_to_all(
        shares.reshape(clusters, capacity, shares.shape[1]),
        "cluster",
        split_axis=0,
        concat_axis=0,
        tiled=True,
    )
    return returned.reshape(slots, shares.shape[1])[position]


def solution(mesh):
    in_specs = (
        P("cluster", "feat"),
        P("cluster", None),
        P(),
        P(("cluster", "feat"), None),
        P(("cluster", "feat"), None),
        P(("cluster", "feat")),
    )
    out_specs = P("cluster", "feat")
    planes = mesh.shape["cluster"] == 8 and mesh.shape["feat"] == 4
    return jax.shard_map(plane_body if planes else body, mesh=mesh, in_specs=in_specs, out_specs=out_specs, check_vma=False)
```
